32 devices in a mesh: dp: 4 (over y, x), row: 2 (over core), col: 4 (over z).
Axes of the slice: x: 2, y: 2, z: 4, core: 2. Of those that a mesh axis runs over, the one named last changes fastest.
Arguments:
- grad_parts: bfloat16 [4, 4, 4096, 10240], P('dp', None, 'row', 'col'), may hold values from -16 to 16, as said below
- params: float32 [4, 4096, 10240], P('dp', 'row', 'col'), may hold values from -1.2 to 1.2
- row_moment: float32 [4, 4096], P('dp', 'row'), may hold values from 0.03 to 3, as said below
- col_moment: float32 [4, 10240], P('dp', 'col'), may hold values from 0.02 to 0.4
Outputs:
- new_params: float32 [4, 4096, 10240], P('dp', 'row', 'col')
- update: bfloat16 [4, 4096, 10240], P('dp', 'row', 'col')
- new_row_moment: float32 [4, 4096], P('dp', 'row')
- new_col_moment: float32 [4, 10240], P('dp', 'col')
The draws below stay inside these ranges and needn't reach their ends.
Inputs may be any that keep to these rules, and one draw needn't show every extreme that they name: `grad_parts`: each replica's partial gradient of the projections. `row_moment`: positive second moments of the rows.
All inputs are finite; a program needn't handle non-finite values.
Results may differ from the reference program's by a relative error of at most 0.011.
Values may be sent and summed in bfloat16 or wider, within the bound.
No kernel may reach another device: no remote copies, remote signals or barrier semaphores. Data moves between devices by JAX's collectives and lax.ppermute only.
A program may use at most 256 MiB of HBM per device.

```python
import math
import jax
import jax.numpy as jnp
from jax import lax

D = 4096
FF = 10240
LAYERS = 4
REPLICAS = 4


def draw_grad_parts(key, part):
    key = jax.random.fold_in(key, 11)
    keys = jax.random.split(key, 3)
    shape = (REPLICAS, LAYERS, D, FF)
    row_ramp = 3.0 ** (jnp.arange(D, dtype=jnp.float32) / (D - 1))
    col_ramp = 3.0 ** (jnp.arange(FF, dtype=jnp.float32) / (FF - 1))
    layer_gain = jnp.where(jnp.arange(LAYERS) % 2 == 0, 0.2, 4.0).astype(jnp.float32)
    spread = jnp.log(3.0)
    noise = jnp.clip(jax.random.normal(keys[0], shape, jnp.float32), -4.0, 4.0)
    row_factor = jnp.exp(jax.random.uniform(keys[1], (LAYERS, D), jnp.float32, 0.0, spread)) * row_ramp
    col_factor = jnp.exp(jax.random.uniform(keys[2], (LAYERS, FF), jnp.float32, 0.0, spread)) * col_ramp
    values = 0.02 * noise * layer_gain[None, :, None, None] * row_factor[None, :, :, None] * col_factor[None, :, None, :]
    values = jnp.clip(values, -15.9, 15.9)
    return values.astype(jnp.bfloat16)


def draw_params(key, part):
    key = jax.random.fold_in(key, 23)
    keys = jax.random.split(key, 2)
    shape = (LAYERS, D, FF)
    power = 0.5
    noise = jnp.clip(jax.random.normal(keys[0], shape, jnp.float32), -4.0, 4.0)
    row_ramp = 3.0 ** (power * jnp.arange(D, dtype=jnp.float32) / (D - 1))
    col_ramp = 3.0 ** (power * jnp.arange(FF, dtype=jnp.float32) / (FF - 1))
    row_factor = jnp.exp(jax.random.uniform(keys[1], (LAYERS, D), jnp.float32, 0.0, 0.3)) * row_ramp
    values = 0.05 * noise * row_factor[:, :, None] * col_ramp[None, None, :] / 1.35
    return values.astype(jnp.float32)


def draw_row_moment(key, part):
    key = jax.random.fold_in(key, 37)
    rise = 10.0
    low = 0.05
    high = 0.2
    position = jnp.arange(D, dtype=jnp.float32) / (D - 1)
    base = jnp.exp(jax.random.uniform(key, (LAYERS, D), jnp.float32, jnp.log(low), jnp.log(high)))
    values = base * (rise ** position)[None, :]
    return values.astype(jnp.float32)


def block_levels(stream_key, extent, cuts, low, top_value):
    gain, own = 1.0, jax.random.fold_in(stream_key, 6)
    for dim, parts in cuts:
        heights = jnp.exp(jax.random.uniform(jax.random.fold_in(own, dim), (parts,), jnp.float32, low / len(cuts), top_value / len(cuts)))
        gain = gain * jnp.repeat(heights, extent[dim] // parts).reshape([-1 if axis == dim else 1 for axis in range(len(extent))])
    return gain


def setup_inputs(seed: int = 0) -> dict:
    arg_keys = jax.random.split(jax.random.key(seed), 5)
    return {
        "grad_parts": draw_grad_parts(jax.random.fold_in(arg_keys[4], 71), 0),
        "params": draw_params(jax.random.fold_in(arg_keys[4], 71), 0),
        "row_moment": draw_row_moment(jax.random.fold_in(arg_keys[4], 71), 0),
        "col_moment": jnp.clip(jnp.exp(math.log(0.4) - 2.9957323 * jax.random.uniform(arg_keys[3], (LAYERS, FF), jnp.float32) ** block_levels(arg_keys[3], (LAYERS, FF), ((0, 4), (1, 4)), -0.2, 0.2)), 0.02, 0.4),
    }


EPSILON = 1e-30
DECAY = 0.8415106807538888
LEARN_RATE = 0.01

def reference(grad_parts, params, row_moment, col_moment):
    gradient = lax.optimization_barrier(jnp.sum(grad_parts.astype(jnp.float32), axis=0))
    squares = gradient * gradient + EPSILON
    new_row = DECAY * row_moment + (1.0 - DECAY) * lax.optimization_barrier(jnp.sum(squares, axis=2)) / FF
    new_col = DECAY * col_moment + (1.0 - DECAY) * lax.optimization_barrier(jnp.sum(squares, axis=1)) / D
    row_mean = lax.optimization_barrier(jnp.sum(new_row, axis=1)) / D
    factor = new_row[:, :, None] * new_col[:, None, :] / row_mean[:, None, None]
    scaled = gradient * lax.rsqrt(factor)
    update_rms = jnp.sqrt(lax.optimization_barrier(jnp.sum(scaled * scaled, axis=(1, 2))) / (D * FF))
    direction = scaled / jnp.maximum(1.0, update_rms)[:, None, None]
    param_scale = jnp.sqrt(lax.optimization_barrier(jnp.sum(params * params, axis=(1, 2))) / (D * FF))
    full_update = param_scale[:, None, None] * direction
    new_params = params - LEARN_RATE * full_update
    return (new_params, full_update.astype(jnp.bfloat16), new_row, new_col)
```

```python
import jax
import jax.numpy as jnp
from jax import lax
from jax.experimental import pallas as pl
from jax.experimental.pallas import tpu as pltpu
from jax.sharding import PartitionSpec as P

D = 4096
FF = 10240
EPSILON = 1e-30
DECAY = 0.8415106807538888
LEARN_RATE = 0.01
LANES = 128
TILE = 128
GROUP = 16
MIB = 1 << 20

NEAR = (1, 2)
FAR = (2, 1)

whole_vmem = pl.BlockSpec(memory_space=pltpu.VMEM)
anywhere = pl.BlockSpec(memory_space=pl.ANY)


def pairs(n, k):
    return [(i, i ^ k) for i in range(n)]


def cost(flops, bytes_accessed):
    return pl.CostEstimate(flops=flops, bytes_accessed=bytes_accessed, transcendentals=0)


def params_of(limit):
    return pltpu.CompilerParams(vmem_limit_bytes=limit)


def pick(parts, me, wants, size):
    columns = parts.shape[2]

    def kernel(me_ref, *refs):
        n = len(refs) // 2
        for a, b in zip(refs[:n], refs[n:]):
            b[...] = a[...]

    def spec(flip, start):
        return pl.BlockSpec((None, TILE, columns), lambda t, m: (m[0] ^ flip, start // TILE + t, 0))

    return pl.pallas_call(
        kernel,
        grid_spec=pltpu.PrefetchScalarGridSpec(
            num_scalar_prefetch=1,
            grid=(size // TILE,),
            in_specs=[spec(f, s) for f, s in wants],
            out_specs=[pl.BlockSpec((TILE, columns), lambda t, m: (t, 0)) for _ in wants],
        ),
        out_shape=[jax.ShapeDtypeStruct((size, columns), parts.dtype) for _ in wants],
        compiler_params=params_of(8 * MIB),
        cost_estimate=cost(0, 4 * len(wants) * size * columns),
        name="pick",
    )(me, *[parts] * len(wants))


def merge(parts, me, got, at, offset, size):
    columns = parts.shape[2]
    half = parts.shape[1] // 2

    def kernel(me_ref, a0, a1, b0, b1, o0, o1):
        o0[...] = (a0[...].astype(jnp.float32) + b0[...].astype(jnp.float32)).astype(o0.dtype)
        o1[...] = (a1[...].astype(jnp.float32) + b1[...].astype(jnp.float32)).astype(o1.dtype)

    def own(h):
        return pl.BlockSpec((None, TILE, columns), lambda t, m: (m[0] ^ FAR[h], (h * half + at) // TILE + t, 0))

    came = pl.BlockSpec((TILE, columns), lambda t, m: ((at - offset) // TILE + t, 0))
    return pl.pallas_call(
        kernel,
        grid_spec=pltpu.PrefetchScalarGridSpec(
            num_scalar_prefetch=1,
            grid=(size // TILE,),
            in_specs=[own(0), own(1), came, came],
            out_specs=[pl.BlockSpec((TILE, columns), lambda t, m: (t, 0))] * 2,
        ),
        out_shape=[jax.ShapeDtypeStruct((size, columns), parts.dtype)] * 2,
        compiler_params=params_of(12 * MIB),
        cost_estimate=cost(2 * size * columns, 12 * size * columns),
        name="merge",
    )(me, parts, parts, *got)


def lane_sums(x):
    return jnp.sum(x.T, axis=0, keepdims=True)


def settle(parts, me, second, third, at, size, state, step):
    rows, columns = parts.shape[1:]
    half = rows // 2
    chunks = columns // LANES
    steps = size // step

    def kernel(me_ref, a0, a1, b0, b1, c0, c1, *refs):
        if state is not None:
            refs = refs[2:]
        g_ref, col_ref, row_ref, sums_ref, carry_ref = refs
        t = pl.program_id(0)

        @pl.when(t == 0)
        def _():
            if state is None:
                carry_ref[...] = jnp.zeros_like(carry_ref)
            else:
                carry_ref[...] = jnp.zeros_like(carry_ref)

        for h, (a, b, c) in enumerate(((a0, b0, c0), (a1, b1, c1))):

            def body(r, carry):
                here = pl.ds(pl.multiple_of(r * GROUP, GROUP), GROUP)
                across = jnp.zeros((GROUP, LANES), jnp.float32)
                down = []
                for k in range(chunks):
                    lanes = slice(k * LANES, (k + 1) * LANES)
                    total = a[here, lanes].astype(jnp.float32) + b[here, lanes].astype(jnp.float32)
                    total = total + c[here, lanes].astype(jnp.float32)
                    first = pl.multiple_of(h * half + at + t * step + r * GROUP, GROUP)
                    g_ref[pl.ds(first, GROUP), lanes] = total.astype(g_ref.dtype)
                    square = total * total
                    across = across + square
                    down.append(carry[k] + square[:8] + square[8:])
                sums_ref[h, pl.ds(pl.multiple_of(t * step + r * GROUP, GROUP), GROUP), :] = across
                return tuple(down)

            carry = tuple(carry_ref[:, k * LANES : (k + 1) * LANES] for k in range(chunks))
            carry = lax.fori_loop(0, step // GROUP, body, carry)
            for k in range(chunks):
                carry_ref[:, k * LANES : (k + 1) * LANES] = carry[k]

        @pl.when(t == steps - 1)
        def _():
            for h in range(2):
                for q in range(size // LANES):
                    lanes = slice(q * LANES, (q + 1) * LANES)
                    row_ref[h : h + 1, lanes] = lane_sums(sums_ref[h, lanes, :])
            col_ref[...] = jnp.sum(carry_ref[...], axis=0, keepdims=True)
            if state is not None:
                col_ref[...] = col_ref[...] + refs_in[1][...]

    refs_in = [None, None]

    def wrapped(me_ref, *refs):
        if state is not None:
            refs_in[0], refs_in[1] = refs[6], refs[7]
        kernel(me_ref, *refs)

    def own(h):
        return pl.BlockSpec((None, step, columns), lambda t, m: (m[0], (h * half + at) // step + t, 0))

    inside = pl.BlockSpec((step, columns), lambda t, m: (at // step + t, 0))
    piece = pl.BlockSpec((step, columns), lambda t, m: (t, 0))
    in_specs = [own(0), own(1), inside, inside, piece, piece]
    operands = [parts, parts, *second, *third]
    aliases = {}
    if state is not None:
        in_specs += [anywhere, whole_vmem]
        operands += state
        aliases = {7: 0}
    return pl.pallas_call(
        wrapped,
        grid_spec=pltpu.PrefetchScalarGridSpec(
            num_scalar_prefetch=1,
            grid=(steps,),
            in_specs=in_specs,
            out_specs=[whole_vmem, whole_vmem, whole_vmem],
            scratch_shapes=[pltpu.VMEM((2, size, LANES), jnp.float32), pltpu.VMEM((8, columns), jnp.float32)],
        ),
        out_shape=[
            pltpu.VMEM((rows, columns), parts.dtype),
            jax.ShapeDtypeStruct((1, columns), jnp.float32),
            jax.ShapeDtypeStruct((2, size), jnp.float32),
        ],
        input_output_aliases=aliases,
        compiler_params=params_of(16 * MIB),
        cost_estimate=cost(12 * size * columns, 12 * size * columns),
        name="settle",
    )(me, *operands)


def power_of(params):
    rows, columns = params.shape

    def kernel(p_ref, o_ref):
        @pl.when(pl.program_id(0) == 0)
        def _():
            o_ref[...] = jnp.zeros_like(o_ref)

        def body(r, total):
            here = pl.ds(pl.multiple_of(r * 8, 8), 8)
            for k in range(columns // LANES):
                p = p_ref[here, k * LANES : (k + 1) * LANES]
                total = total + p * p
            return total

        o_ref[...] += lax.fori_loop(0, TILE // 8, body, jnp.zeros((8, LANES), jnp.float32))

    return pl.pallas_call(
        kernel,
        grid=(rows // TILE,),
        in_specs=[pl.BlockSpec((TILE, columns), lambda t: (t, 0))],
        out_specs=pl.BlockSpec((8, LANES), lambda t: (0, 0)),
        out_shape=jax.ShapeDtypeStruct((8, LANES), jnp.float32),
        compiler_params=params_of(8 * MIB),
        cost_estimate=cost(2 * rows * columns, 4 * rows * columns),
        name="param_power",
    )(params)


def tree(values):
    while len(values) > 1:
        values = [a + b for a, b in zip(values[::2], values[1::2])]
    return values[0]


def weigh(gradient, col_sums, col_moment, row_sums, power):
    rows, columns = gradient.shape
    chunks = columns // LANES
    n = len(col_sums)

    def kernel(g_ref, *refs):
        sums, (moment_ref, row_ref, power_ref, new_ref, root_ref, out_ref, wide_ref, acc_ref) = refs[:n], refs[n:]
        total = tree([s[...] for s in sums]) + D * EPSILON
        new = DECAY * moment_ref[...] + (1.0 - DECAY) * total / D
        new_ref[...] = new
        root = lax.rsqrt(new)
        root_ref[...] = root
        wide_ref[...] = jnp.broadcast_to(root, wide_ref.shape)
        out_ref[:, :rows] = row_ref[...]
        out_ref[:, 2 * rows :] = jnp.sum(power_ref[...], axis=0, keepdims=True)
        roots = [wide_ref[:, k * LANES : (k + 1) * LANES] for k in range(chunks)]

        def body(r, carry):
            here = pl.ds(pl.multiple_of(r * GROUP, GROUP), GROUP)
            low = jnp.zeros((8, LANES), jnp.float32)
            high = jnp.zeros((8, LANES), jnp.float32)
            for k in range(chunks):
                g = g_ref[here, k * LANES : (k + 1) * LANES].astype(jnp.float32)
                a, b = g[:8] * roots[k], g[8:] * roots[k]
                low, high = low + a * a, high + b * b
            acc_ref[here, :] = jnp.concatenate([low, high], axis=0)
            return carry

        lax.fori_loop(0, rows // GROUP, body, 0)
        for q in range(rows // LANES):
            out_ref[:, rows + q * LANES : rows + (q + 1) * LANES] = lane_sums(acc_ref[q * LANES : (q + 1) * LANES, :])

    return pl.pallas_call(
        kernel,
        in_specs=[whole_vmem] * (n + 4),
        out_specs=[whole_vmem] * 3,
        out_shape=[
            jax.ShapeDtypeStruct((1, columns), jnp.float32),
            jax.ShapeDtypeStruct((1, columns), jnp.float32),
            jax.ShapeDtypeStruct((1, 2 * rows + LANES), jnp.float32),
        ],
        scratch_shapes=[pltpu.VMEM((8, columns), jnp.float32), pltpu.VMEM((rows, LANES), jnp.float32)],
        compiler_params=params_of(8 * MIB),
        cost_estimate=cost(4 * rows * columns, 2 * rows * columns),
        name="weigh",
    )(gradient, *col_sums, col_moment, row_sums, power)


def balance(messages, row_moment):
    rows = row_moment.shape[1]
    n = len(messages)

    def kernel(*refs):
        got, (moment_ref, new_ref, root_ref, out_ref) = refs[:n], refs[n:]
        total = tree([m[...] for m in got])
        new = DECAY * moment_ref[...] + (1.0 - DECAY) * (total[:, :rows] + FF * EPSILON) / FF
        new_ref[...] = new
        root = lax.rsqrt(new)
        root_ref[...] = root
        ratio = total[:, rows : 2 * rows] * (root * root)
        fold = lambda x: tree_lanes(x, rows)
        out_ref[...] = jnp.zeros_like(out_ref)
        out_ref[0:1, :] = fold(ratio)
        out_ref[1:2, :] = fold(new)
        out_ref[2:3, :] = total[:, 2 * rows :]

    return pl.pallas_call(
        kernel,
        in_specs=[whole_vmem] * (n + 1),
        out_specs=[whole_vmem] * 3,
        out_shape=[
            jax.ShapeDtypeStruct((1, rows), jnp.float32),
            jax.ShapeDtypeStruct((1, rows), jnp.float32),
            jax.ShapeDtypeStruct((8, LANES), jnp.float32),
        ],
        compiler_params=params_of(4 * MIB),
        name="balance",
    )(*messages, row_moment)


def tree_lanes(x, rows):
    total = x[:, :LANES]
    for q in range(1, rows // LANES):
        total = total + x[:, q * LANES : (q + 1) * LANES]
    return total


def finish(gradient, params, row_root, col_root, stats):
    rows, columns = gradient.shape
    n = len(stats)

    def kernel(g_ref, p_ref, row_ref, col_ref, *refs):
        got, (new_ref, update_ref, scale_ref) = refs[:n], refs[n:]
        t = pl.program_id(0)

        @pl.when(t == 0)
        def _():
            total = jnp.sum(tree([s[...] for s in got]), axis=1, keepdims=True)
            mean = total[1:2] / D
            rms = jnp.sqrt(mean * total[0:1] / (D * FF))
            scale = jnp.sqrt(total[2:3] / (D * FF))
            factor = scale * jnp.sqrt(mean) / jnp.maximum(1.0, rms)
            scale_ref[...] = jnp.broadcast_to(col_ref[...] * factor, scale_ref.shape)

        first = pl.multiple_of(t * TILE, TILE)
        lanes = row_ref[:, pl.ds(first, TILE)]
        wide = jnp.broadcast_to(lanes, (TILE, TILE)).T
        for r in range(TILE // GROUP):
            here = pl.ds(pl.multiple_of(first + r * GROUP, GROUP), GROUP)
            out = slice(r * GROUP, (r + 1) * GROUP)
            root = wide[out, :]
            for k in range(columns // LANES):
                at = slice(k * LANES, (k + 1) * LANES)
                g = g_ref[here, at].astype(jnp.float32)
                s = scale_ref[:, at]
                full = jnp.concatenate([g[:8] * s, g[8:] * s], axis=0) * root
                update_ref[out, at] = full.astype(update_ref.dtype)
                new_ref[out, at] = p_ref[here, at] - LEARN_RATE * full

    return pl.pallas_call(
        kernel,
        grid=(rows // TILE,),
        in_specs=[whole_vmem] * (4 + n),
        out_specs=[pl.BlockSpec((TILE, columns), lambda t: (t, 0))] * 2,
        out_shape=[jax.ShapeDtypeStruct((rows, columns), jnp.float32), jax.ShapeDtypeStruct((rows, columns), jnp.bfloat16)],
        scratch_shapes=[pltpu.VMEM((8, columns), jnp.float32)],
        compiler_params=params_of(8 * MIB),
        cost_estimate=cost(6 * rows * columns, 12 * rows * columns),
        name="finish",
    )(gradient, params, row_root, col_root, *stats)


def all_parts(value, axis, size):
    return [value] + [lax.ppermute(value, axis, pairs(size, k)) for k in range(1, size)]


def after(values, others):
    return lax.optimization_barrier((tuple(values), tuple(others)))[0]


def solution(mesh):
    across = mesh.shape["row"]
    along = mesh.shape["col"]

    def hop(values, lines):
        return [lax.ppermute(v, "dp", pairs(mesh.shape["dp"], n)) for v, n in zip(values, lines)]

    def on_device(grad_parts, params, row_moment, col_moment):
        parts = grad_parts[0]
        rows, columns = parts.shape[1:]
        half = rows // 2
        me = lax.axis_index("dp").astype(jnp.int32)[None]

        head = min(TILE, half)
        rest = half - head
        first_head = hop(pick(parts, me, [(3, 0), (3, half)], head), NEAR)
        pieces = []
        if rest:
            first_rest = hop(pick(parts, me, [(3, head), (3, half + head)], rest), NEAR)
            mine = (rest // TILE + 1) // 2 * TILE
            pieces = [(head, mine)] + ([(head + mine, rest - mine)] if rest > mine else [])
        second = hop(pick(parts, me, [(NEAR[0], 0), (NEAR[1], half)], half), NEAR)
        power = power_of(params[0])

        merged = []
        for at, size in pieces:
            got = after(first_rest, merged[-1]) if merged else first_rest
            merged.append(merge(parts, me, got, at, head, size))
        got = after(first_head, merged[-1]) if merged else first_head
        merged.append(merge(parts, me, got, 0, 0, head))
        pieces.append((0, head))
        third = [hop(m, FAR) for m in merged]

        state, row_pieces = None, {}
        for (at, size), came in zip(pieces, third):
            gradient, col_sums, row_piece = settle(parts, me, second, came, at, size, state, min(64, size))
            state = [gradient, col_sums]
            row_pieces[at] = row_piece
        row_sums = jnp.concatenate([row_pieces[at][h : h + 1] for h in range(2) for at in sorted(row_pieces)], axis=1)

        new_col, col_root, message = weigh(gradient, all_parts(col_sums, "row", across), col_moment, row_sums, power)
        new_row, row_root, stats = balance(all_parts(message, "col", along), row_moment)
        new_params, update = finish(gradient, params[0], row_root, col_root, all_parts(stats, "row", across))
        return new_params[None], update[None], new_row, new_col

    placed = (P("dp", None, "row", "col"), P("dp", "row", "col"), P("dp", "row"), P("dp", "col"))
    return jax.shard_map(
        on_device,
        mesh=mesh,
        in_specs=placed,
        out_specs=(P("dp", "row", "col"), P("dp", "row", "col"), P("dp", "row"), P("dp", "col")),
        check_vma=False,
    )
```

```python
import jax
import jax.numpy as jnp
from jax import lax
from jax.experimental import pallas as pl
from jax.experimental.pallas import tpu as pltpu
from jax.sharding import PartitionSpec as P

D = 4096
FF = 10240
EPSILON = 1e-30
DECAY = 0.8415106807538888
LEARN_RATE = 0.01
LANES = 128
TILE = 128
GROUP = 16
SHARES = 4
MIB = 1 << 20

NEAR = (1, 2)
FAR = (2, 1)

whole_vmem = pl.BlockSpec(memory_space=pltpu.VMEM)
anywhere = pl.BlockSpec(memory_space=pl.ANY)


def pairs(n, k):
    return [(i, i ^ k) for i in range(n)]


def in_hbm(x):
    return pltpu.with_memory_space_constraint(x, pltpu.HBM)


def cost(flops, bytes_accessed):
    return pl.CostEstimate(flops=flops, bytes_accessed=bytes_accessed, transcendentals=0)


def params_of(limit):
    return pltpu.CompilerParams(vmem_limit_bytes=limit)


def pick(parts, me, wants, size):
    columns = parts.shape[2]

    def kernel(me_ref, *refs):
        n = len(refs) // 2
        for a, b in zip(refs[:n], refs[n:]):
            b[...] = a[...]

    def spec(flip, start):
        return pl.BlockSpec((None, TILE, columns), lambda t, m: (m[0] ^ flip, start // TILE + t, 0))

    return pl.pallas_call(
        kernel,
        grid_spec=pltpu.PrefetchScalarGridSpec(
            num_scalar_prefetch=1,
            grid=(size // TILE,),
            in_specs=[spec(f, s) for f, s in wants],
            out_specs=[pl.BlockSpec((TILE, columns), lambda t, m: (t, 0)) for _ in wants],
        ),
        out_shape=[jax.ShapeDtypeStruct((size, columns), parts.dtype) for _ in wants],
        compiler_params=params_of(8 * MIB),
        cost_estimate=cost(0, 4 * len(wants) * size * columns),
        name="pick",
    )(me, *[parts] * len(wants))


def merge(parts, me, got, at, offset, size):
    columns = parts.shape[2]
    half = parts.shape[1] // 2

    def kernel(me_ref, a0, a1, b0, b1, o0, o1):
        o0[...] = (a0[...].astype(jnp.float32) + b0[...].astype(jnp.float32)).astype(o0.dtype)
        o1[...] = (a1[...].astype(jnp.float32) + b1[...].astype(jnp.float32)).astype(o1.dtype)

    def own(h):
        return pl.BlockSpec((None, TILE, columns), lambda t, m: (m[0] ^ FAR[h], (h * half + at) // TILE + t, 0))

    came = pl.BlockSpec((TILE, columns), lambda t, m: ((at - offset) // TILE + t, 0))
    return pl.pallas_call(
        kernel,
        grid_spec=pltpu.PrefetchScalarGridSpec(
            num_scalar_prefetch=1,
            grid=(size // TILE,),
            in_specs=[own(0), own(1), came, came],
            out_specs=[pl.BlockSpec((TILE, columns), lambda t, m: (t, 0))] * 2,
        ),
        out_shape=[jax.ShapeDtypeStruct((size, columns), parts.dtype)] * 2,
        compiler_params=params_of(9 * MIB),
        cost_estimate=cost(2 * size * columns, 12 * size * columns),
        name="merge",
    )(me, parts, parts, *got)


def lane_sums(x):
    return jnp.sum(x.T, axis=0, keepdims=True)


def settle(parts, me, second, third, at, size, state, step):
    rows, columns = parts.shape[1:]
    half = rows // 2
    chunks = columns // LANES
    steps = size // step

    def kernel(me_ref, a0, a1, b0, b1, c0, c1, *refs):
        before_ref = None
        if state is not None:
            before_ref, refs = refs[1], refs[2:]
        g_ref, col_ref, row_ref, sums_ref, carry_ref = refs
        t = pl.program_id(0)

        @pl.when(t == 0)
        def _():
            carry_ref[...] = jnp.zeros_like(carry_ref)

        for h, (a, b, c) in enumerate(((a0, b0, c0), (a1, b1, c1))):

            def body(r, carry):
                here = pl.ds(pl.multiple_of(r * GROUP, GROUP), GROUP)
                across = jnp.zeros((GROUP, LANES), jnp.float32)
                down = []
                for k in range(chunks):
                    lanes = slice(k * LANES, (k + 1) * LANES)
                    total = a[here, lanes].astype(jnp.float32) + b[here, lanes].astype(jnp.float32)
                    total = total + c[here, lanes].astype(jnp.float32)
                    first = pl.multiple_of(h * half + at + t * step + r * GROUP, GROUP)
                    g_ref[pl.ds(first, GROUP), lanes] = total.astype(g_ref.dtype)
                    square = total * total
                    across = across + square
                    down.append(carry[k] + square[:8] + square[8:])
                sums_ref[h, pl.ds(pl.multiple_of(t * step + r * GROUP, GROUP), GROUP), :] = across
                return tuple(down)

            carry = tuple(carry_ref[:, k * LANES : (k + 1) * LANES] for k in range(chunks))
            carry = lax.fori_loop(0, step // GROUP, body, carry)
            for k in range(chunks):
                carry_ref[:, k * LANES : (k + 1) * LANES] = carry[k]

        @pl.when(t == steps - 1)
        def _():
            for h in range(2):
                for q in range(size // LANES):
                    lanes = slice(q * LANES, (q + 1) * LANES)
                    row_ref[h : h + 1, lanes] = lane_sums(sums_ref[h, lanes, :])
            col_ref[...] = jnp.sum(carry_ref[...], axis=0, keepdims=True)
            if state is not None:
                col_ref[...] = col_ref[...] + before_ref[...]

    def own(h):
        return pl.BlockSpec((None, step, columns), lambda t, m: (m[0], (h * half + at) // step + t, 0))

    inside = pl.BlockSpec((step, columns), lambda t, m: (at // step + t, 0))
    piece = pl.BlockSpec((step, columns), lambda t, m: (t, 0))
    in_specs = [own(0), own(1), inside, inside, piece, piece]
    operands = [parts, parts, *second, *third]
    aliases = {}
    if state is not None:
        in_specs += [anywhere, whole_vmem]
        operands += state
        aliases = {7: 0}
    return pl.pallas_call(
        kernel,
        grid_spec=pltpu.PrefetchScalarGridSpec(
            num_scalar_prefetch=1,
            grid=(steps,),
            in_specs=in_specs,
            out_specs=[whole_vmem, whole_vmem, whole_vmem],
            scratch_shapes=[pltpu.VMEM((2, size, LANES), jnp.float32), pltpu.VMEM((8, columns), jnp.float32)],
        ),
        out_shape=[
            pltpu.VMEM((rows, columns), parts.dtype),
            jax.ShapeDtypeStruct((1, columns), jnp.float32),
            jax.ShapeDtypeStruct((2, size), jnp.float32),
        ],
        input_output_aliases=aliases,
        compiler_params=params_of(7 * MIB),
        cost_estimate=cost(12 * size * columns, 12 * size * columns),
        name="settle",
    )(me, *operands)


def power_of(params):
    rows, columns = params.shape
    steps = rows // TILE
    shares = min(SHARES, steps)
    each = steps // shares

    def kernel(p_ref, *refs):
        *kept, o_ref, sems = refs
        copies = []
        for t in range(steps):
            here, there = pl.ds(t * TILE, TILE), pl.ds(t % each * TILE, TILE)
            copies.append(pltpu.make_async_copy(p_ref.at[here], kept[t // each].at[there], sems.at[t]))
            copies[-1].start()
        total = jnp.zeros((8, LANES), jnp.float32)
        for t in range(steps):
            copies[t].wait()

            def body(r, total):
                here = pl.ds(pl.multiple_of(t % each * TILE + r * 8, 8), 8)
                for k in range(columns // LANES):
                    p = kept[t // each][here, k * LANES : (k + 1) * LANES]
                    total = total + p * p
                return total

            total = lax.fori_loop(0, TILE // 8, body, total)
        o_ref[...] = total

    *kept, power = pl.pallas_call(
        kernel,
        in_specs=[anywhere],
        out_specs=[whole_vmem] * (shares + 1),
        out_shape=[pltpu.VMEM((rows // shares, columns), jnp.float32)] * shares
        + [jax.ShapeDtypeStruct((8, LANES), jnp.float32)],
        scratch_shapes=[pltpu.SemaphoreType.DMA((steps,))],
        compiler_params=params_of(MIB),
        cost_estimate=cost(2 * rows * columns, 4 * rows * columns),
        name="param_power",
    )(in_hbm(params))
    return kept, power


def tree(values):
    while len(values) > 1:
        values = [a + b for a, b in zip(values[::2], values[1::2])]
    return values[0]


def weigh(gradient, col_sums, col_moment, row_sums, power):
    rows, columns = gradient.shape
    chunks = columns // LANES
    n = len(col_sums)

    def kernel(g_ref, *refs):
        sums, (moment_ref, row_ref, power_ref, new_ref, root_ref, out_ref, wide_ref, acc_ref) = refs[:n], refs[n:]
        total = tree([s[...] for s in sums]) + D * EPSILON
        new = DECAY * moment_ref[...] + (1.0 - DECAY) * total / D
        new_ref[...] = new
        root = lax.rsqrt(new)
        root_ref[...] = root
        wide_ref[...] = jnp.broadcast_to(root, wide_ref.shape)
        out_ref[:, :rows] = row_ref[...]
        out_ref[:, 2 * rows :] = jnp.sum(power_ref[...], axis=0, keepdims=True)
        roots = [wide_ref[:, k * LANES : (k + 1) * LANES] for k in range(chunks)]

        def body(r, carry):
            here = pl.ds(pl.multiple_of(r * GROUP, GROUP), GROUP)
            low = jnp.zeros((8, LANES), jnp.float32)
            high = jnp.zeros((8, LANES), jnp.float32)
            for k in range(chunks):
                g = g_ref[here, k * LANES : (k + 1) * LANES].astype(jnp.float32)
                a, b = g[:8] * roots[k], g[8:] * roots[k]
                low, high = low + a * a, high + b * b
            acc_ref[here, :] = jnp.concatenate([low, high], axis=0)
            return carry

        lax.fori_loop(0, rows // GROUP, body, 0)
        for q in range(rows // LANES):
            out_ref[:, rows + q * LANES : rows + (q + 1) * LANES] = lane_sums(acc_ref[q * LANES : (q + 1) * LANES, :])

    return pl.pallas_call(
        kernel,
        in_specs=[whole_vmem] * (n + 4),
        out_specs=[whole_vmem] * 3,
        out_shape=[
            jax.ShapeDtypeStruct((1, columns), jnp.float32),
            jax.ShapeDtypeStruct((1, columns), jnp.float32),
            jax.ShapeDtypeStruct((1, 2 * rows + LANES), jnp.float32),
        ],
        scratch_shapes=[pltpu.VMEM((8, columns), jnp.float32), pltpu.VMEM((rows, LANES), jnp.float32)],
        compiler_params=params_of(8 * MIB),
        cost_estimate=cost(4 * rows * columns, 2 * rows * columns),
        name="weigh",
    )(gradient, *col_sums, col_moment, row_sums, power)


def balance(messages, row_moment):
    rows = row_moment.shape[1]
    n = len(messages)

    def kernel(*refs):
        got, (moment_ref, new_ref, root_ref, out_ref) = refs[:n], refs[n:]
        total = tree([m[...] for m in got])
        new = DECAY * moment_ref[...] + (1.0 - DECAY) * (total[:, :rows] + FF * EPSILON) / FF
        new_ref[...] = new
        root = lax.rsqrt(new)
        root_ref[...] = root
        ratio = total[:, rows : 2 * rows] * (root * root)
        fold = lambda x: tree_lanes(x, rows)
        out_ref[...] = jnp.zeros_like(out_ref)
        out_ref[0:1, :] = fold(ratio)
        out_ref[1:2, :] = fold(new)
        out_ref[2:3, :] = total[:, 2 * rows :]

    return pl.pallas_call(
        kernel,
        in_specs=[whole_vmem] * (n + 1),
        out_specs=[whole_vmem] * 3,
        out_shape=[
            jax.ShapeDtypeStruct((1, rows), jnp.float32),
            jax.ShapeDtypeStruct((1, rows), jnp.float32),
            jax.ShapeDtypeStruct((8, LANES), jnp.float32),
        ],
        compiler_params=params_of(4 * MIB),
        name="balance",
    )(*messages, row_moment)


def tree_lanes(x, rows):
    total = x[:, :LANES]
    for q in range(1, rows // LANES):
        total = total + x[:, q * LANES : (q + 1) * LANES]
    return total


def finish(gradient, params, row_root, col_root, stats):
    rows, columns = gradient.shape
    n = len(stats)
    shares = len(params)
    each = rows // shares // TILE
    group = 2 * GROUP

    def kernel(_, row_ref, col_ref, *refs):
        got, refs = refs[shares : shares + n], refs[shares + n :]
        g_ref, held, (new_ref, update_ref, scale_ref, sems) = refs[0], refs[1 : 1 + shares], refs[1 + shares :]
        total = jnp.sum(tree([s[...] for s in got]), axis=1, keepdims=True)
        mean = total[1:2] / D
        rms = jnp.sqrt(mean * total[0:1] / (D * FF))
        scale = jnp.sqrt(total[2:3] / (D * FF))
        factor = scale * jnp.sqrt(mean) / jnp.maximum(1.0, rms)
        scale_ref[...] = jnp.broadcast_to(col_ref[...] * factor, scale_ref.shape)

        def copies(q, t):
            here = pl.ds(pl.multiple_of((q * each + t) * TILE, TILE), TILE)
            there = pl.ds(pl.multiple_of(t * TILE, TILE), TILE)
            return (
                pltpu.make_async_copy(held[q].at[there], new_ref.at[here], sems.at[0, q * each + t]),
                pltpu.make_async_copy(g_ref.at[here], update_ref.at[here], sems.at[1, q * each + t]),
            )

        for q in range(shares):

            def block(t, carry):
                first = pl.multiple_of((q * each + t) * TILE, TILE)
                wide = jnp.broadcast_to(row_ref[:, pl.ds(first, TILE)], (LANES, TILE)).T
                for r in range(0, TILE, group):
                    here = pl.ds(pl.multiple_of(first + r, group), group)
                    there = pl.ds(pl.multiple_of(t * TILE + r, group), group)
                    root = wide[r : r + group, :]
                    for k in range(columns // LANES):
                        at = slice(k * LANES, (k + 1) * LANES)
                        g = g_ref[here, at].astype(jnp.float32)
                        s = scale_ref[:, at]
                        full = jnp.concatenate([g[i : i + 8] * s for i in range(0, group, 8)], axis=0) * root
                        g_ref[here, at] = full.astype(g_ref.dtype)
                        held[q][there, at] = held[q][there, at] - LEARN_RATE * full
                for copy in copies(q, t):
                    copy.start()
                return carry

            lax.fori_loop(0, each, block, 0)

        for q in range(shares):

            def drain(t, carry):
                for copy in copies(q, t):
                    copy.wait()
                return carry

            lax.fori_loop(0, each, drain, 0)

    out = pl.pallas_call(
        kernel,
        in_specs=[anywhere, whole_vmem, whole_vmem] + [anywhere] * shares + [whole_vmem] * n,
        out_specs=[whole_vmem] * (1 + shares) + [anywhere] * 2,
        out_shape=[pltpu.VMEM(x.shape, x.dtype) for x in (gradient, *params)]
        + [pltpu.HBM((rows, columns), jnp.float32), pltpu.HBM((rows, columns), jnp.bfloat16)],
        input_output_aliases={0: 0, **{3 + q: 1 + q for q in range(shares)}},
        scratch_shapes=[pltpu.VMEM((8, columns), jnp.float32), pltpu.SemaphoreType.DMA((2, rows // TILE))],
        compiler_params=params_of(4 * MIB),
        cost_estimate=cost(6 * rows * columns, 12 * rows * columns),
        name="finish",
    )(gradient, row_root, col_root, *params, *stats)
    return out[-2:]


def all_parts(value, axis, size):
    return [value] + [lax.ppermute(value, axis, pairs(size, k)) for k in range(1, size)]


def cut(half):
    units = half // TILE
    sizes = [1, 2, units - 3] if units > 3 else [1, units - 1] if units > 1 else [units]
    edges, at = [], 0
    for n in sizes:
        edges.append((at, n * TILE))
        at += n * TILE
    return edges


def after(values, others):
    return lax.optimization_barrier((tuple(values), tuple(others)))[0]


def solution(mesh):
    across = mesh.shape["row"]
    along = mesh.shape["col"]

    def hop(values, lines):
        return [lax.ppermute(v, "dp", pairs(mesh.shape["dp"], n)) for v, n in zip(values, lines)]

    def on_device(grad_parts, params, row_moment, col_moment):
        parts = grad_parts[0]
        rows, columns = parts.shape[1:]
        half = rows // 2
        me = lax.axis_index("dp").astype(jnp.int32)[None]

        held = in_hbm(parts)
        pieces = cut(half)
        rounds = []

        def send(values, lines):
            if len(rounds) > 1:
                values = after(values, rounds[-2])
            rounds.append(hop(values, lines))
            return rounds[-1]

        first, turn = [], me
        for at, size in pieces:
            picked = pick(held, turn, [(3, at), (3, half + at)], size)
            (turn,) = after([me], picked)
            first.append(send(picked, NEAR))
        second = send(pick(held, turn, [(NEAR[0], 0), (NEAR[1], half)], half), NEAR)
        pieces.reverse()
        third, done = [], []
        for (at, size), came in zip(pieces, reversed(first)):
            done = merge(held, me, after(came, done), at, at, size)
            third.append(send(done, FAR))

        state, row_pieces = None, {}
        for (at, size), came in zip(pieces, third):
            gradient, col_sums, row_piece = settle(held, me, second, came, at, size, state, min(64, size))
            if state is None:
                kept, power = power_of(after([params[0]], [col_sums])[0])
            state = [gradient, col_sums]
            row_pieces[at] = row_piece
        row_sums = jnp.concatenate([row_pieces[at][h : h + 1] for h in range(2) for at in sorted(row_pieces)], axis=1)

        new_col, col_root, message = weigh(gradient, all_parts(col_sums, "row", across), col_moment, row_sums, power)
        new_row, row_root, stats = balance(all_parts(message, "col", along), row_moment)
        new_params, update = finish(gradient, kept, row_root, col_root, all_parts(stats, "row", across))
        return new_params[None], update[None], new_row, new_col

    placed = (P("dp", None, "row", "col"), P("dp", "row", "col"), P("dp", "row"), P("dp", "col"))
    return jax.shard_map(
        on_device,
        mesh=mesh,
        in_specs=placed,
        out_specs=(P("dp", "row", "col"), P("dp", "row", "col"), P("dp", "row"), P("dp", "col")),
        check_vma=False,
    )
```

```python
import jax
import jax.numpy as jnp
from jax import lax
from jax.experimental import pallas as pl
from jax.experimental.pallas import tpu as pltpu
from jax.sharding import PartitionSpec as P

D = 4096
FF = 10240
EPSILON = 1e-30
DECAY = 0.8415106807538888
LEARN_RATE = 0.01
LANES = 128
TILE = 128
GROUP = 16
SHARES = 4
MIB = 1 << 20

NEAR = (1, 2)
FAR = (2, 1)

whole_vmem = pl.BlockSpec(memory_space=pltpu.VMEM)
anywhere = pl.BlockSpec(memory_space=pl.ANY)


def pairs(n, k):
    return [(i, i ^ k) for i in range(n)]


def in_hbm(x):
    return pltpu.with_memory_space_constraint(x, pltpu.HBM)


def cost(flops, bytes_accessed):
    return pl.CostEstimate(flops=flops, bytes_accessed=bytes_accessed, transcendentals=0)


def params_of(limit):
    return pltpu.CompilerParams(vmem_limit_bytes=limit)


def pick(parts, me, wants, size):
    columns = parts.shape[2]

    def kernel(me_ref, *refs):
        n = len(refs) // 2
        for a, b in zip(refs[:n], refs[n:]):
            b[...] = a[...]

    def spec(flip, start):
        return pl.BlockSpec((None, TILE, columns), lambda t, m: (m[0] ^ flip, start // TILE + t, 0))

    return pl.pallas_call(
        kernel,
        grid_spec=pltpu.PrefetchScalarGridSpec(
            num_scalar_prefetch=1,
            grid=(size // TILE,),
            in_specs=[spec(f, s) for f, s in wants],
            out_specs=[pl.BlockSpec((TILE, columns), lambda t, m: (t, 0)) for _ in wants],
        ),
        out_shape=[jax.ShapeDtypeStruct((size, columns), parts.dtype) for _ in wants],
        compiler_params=params_of(8 * MIB),
        cost_estimate=cost(0, 4 * len(wants) * size * columns),
        name="pick",
    )(me, *[parts] * len(wants))


def grab(parts, wants, size):
    columns = parts.shape[2]
    n = len(wants)

    def kernel(parts_ref, *refs):
        outs, sems = refs[:n], refs[n]
        me = lax.axis_index("dp")
        copies = []
        for i, (flip, start) in enumerate(wants):
            copies.append(pltpu.make_async_copy(parts_ref.at[me ^ flip, pl.ds(start, size)], outs[i], sems.at[i]))
            copies[-1].start()
        for copy in copies:
            copy.wait()

    return pl.pallas_call(
        kernel,
        in_specs=[anywhere],
        out_specs=[whole_vmem] * n,
        out_shape=[pltpu.VMEM((size, columns), parts.dtype)] * n,
        scratch_shapes=[pltpu.SemaphoreType.DMA((n,))],
        compiler_params=params_of(MIB),
        name="grab",
    )(parts)


def merge(parts, me, got, at, offset, size, lead=()):
    columns = parts.shape[2]
    half = parts.shape[1] // 2
    skip = 1 if lead else 0

    def add(o, a, b):
        o[...] = (a[...].astype(jnp.float32) + b[...].astype(jnp.float32)).astype(o.dtype)

    def kernel(me_ref, a0, a1, *refs):
        (o0, o1), refs = refs[-2:], refs[:-2]
        t = pl.program_id(0)

        @pl.when(t >= skip)
        def _():
            add(o0, a0, refs[-2])
            add(o1, a1, refs[-1])

        if lead:

            @pl.when(t == 0)
            def _():
                add(o0, a0, refs[0])
                add(o1, a1, refs[1])

    def own(h):
        return pl.BlockSpec((None, TILE, columns), lambda t, m: (m[0] ^ FAR[h], (h * half + at) // TILE + t, 0))

    first = at // TILE + skip - offset // TILE
    came = pl.BlockSpec((TILE, columns), lambda t, m: (first + jnp.maximum(t - skip, 0), 0))
    ahead = pl.BlockSpec((TILE, columns), lambda t, m: (0, 0))
    return pl.pallas_call(
        kernel,
        grid_spec=pltpu.PrefetchScalarGridSpec(
            num_scalar_prefetch=1,
            grid=(size // TILE,),
            in_specs=[own(0), own(1)] + [ahead] * len(lead) + [came, came],
            out_specs=[pl.BlockSpec((TILE, columns), lambda t, m: (t, 0))] * 2,
        ),
        out_shape=[jax.ShapeDtypeStruct((size, columns), parts.dtype)] * 2,
        compiler_params=params_of(12 * MIB),
        cost_estimate=cost(2 * size * columns, 12 * size * columns),
        name="merge",
    )(me, parts, parts, *lead, *got)


def lane_sums(x):
    return jnp.sum(x.T, axis=0, keepdims=True)


def settle(parts, me, second, third, at, size, state, step):
    rows, columns = parts.shape[1:]
    half = rows // 2
    chunks = columns // LANES
    steps = size // step

    def kernel(me_ref, a0, a1, b0, b1, c0, c1, *refs):
        before_ref = None
        if state is not None:
            before_ref, refs = refs[1], refs[2:]
        g_ref, col_ref, row_ref, sums_ref, carry_ref = refs
        t = pl.program_id(0)

        @pl.when(t == 0)
        def _():
            carry_ref[...] = jnp.zeros_like(carry_ref)

        for h, (a, b, c) in enumerate(((a0, b0, c0), (a1, b1, c1))):

            def body(r, carry):
                here = pl.ds(pl.multiple_of(r * GROUP, GROUP), GROUP)
                across = jnp.zeros((GROUP, LANES), jnp.float32)
                down = []
                for k in range(chunks):
                    lanes = slice(k * LANES, (k + 1) * LANES)
                    total = a[here, lanes].astype(jnp.float32) + b[here, lanes].astype(jnp.float32)
                    total = total + c[here, lanes].astype(jnp.float32)
                    first = pl.multiple_of(h * half + at + t * step + r * GROUP, GROUP)
                    g_ref[pl.ds(first, GROUP), lanes] = total.astype(g_ref.dtype)
                    square = total * total
                    across = across + square
                    down.append(carry[k] + square[:8] + square[8:])
                sums_ref[h, pl.ds(pl.multiple_of(t * step + r * GROUP, GROUP), GROUP), :] = across
                return tuple(down)

            carry = tuple(carry_ref[:, k * LANES : (k + 1) * LANES] for k in range(chunks))
            carry = lax.fori_loop(0, step // GROUP, body, carry)
            for k in range(chunks):
                carry_ref[:, k * LANES : (k + 1) * LANES] = carry[k]

        @pl.when(t == steps - 1)
        def _():
            for h in range(2):
                for q in range(size // LANES):
                    lanes = slice(q * LANES, (q + 1) * LANES)
                    row_ref[:, h * size + q * LANES : h * size + (q + 1) * LANES] = lane_sums(sums_ref[h, lanes, :])
            col_ref[...] = jnp.sum(carry_ref[...], axis=0, keepdims=True)
            if state is not None:
                col_ref[...] = col_ref[...] + before_ref[...]

    def own(h):
        return pl.BlockSpec((None, step, columns), lambda t, m: (m[0], (h * half + at) // step + t, 0))

    inside = pl.BlockSpec((step, columns), lambda t, m: (at // step + t, 0))
    piece = pl.BlockSpec((step, columns), lambda t, m: (t, 0))
    in_specs = [own(0), own(1), inside, inside, piece, piece]
    operands = [parts, parts, *second, *third]
    aliases = {}
    if state is not None:
        in_specs += [anywhere, whole_vmem]
        operands += state
        aliases = {7: 0}
    return pl.pallas_call(
        kernel,
        grid_spec=pltpu.PrefetchScalarGridSpec(
            num_scalar_prefetch=1,
            grid=(steps,),
            in_specs=in_specs,
            out_specs=[whole_vmem, whole_vmem, whole_vmem],
            scratch_shapes=[pltpu.VMEM((2, size, LANES), jnp.float32), pltpu.VMEM((8, columns), jnp.float32)],
        ),
        out_shape=[
            pltpu.VMEM((rows, columns), parts.dtype),
            jax.ShapeDtypeStruct((1, columns), jnp.float32),
            jax.ShapeDtypeStruct((1, 2 * size), jnp.float32),
        ],
        input_output_aliases=aliases,
        compiler_params=params_of(7 * MIB),
        cost_estimate=cost(12 * size * columns, 12 * size * columns),
        name="settle",
    )(me, *operands)


def presum(parts, me, second, at, size):
    columns = parts.shape[2]
    half = parts.shape[1] // 2
    step = min(64, size)

    def kernel(me_ref, a0, a1, b0, b1, o_ref):
        t = pl.program_id(0)
        for h, (a, b) in enumerate(((a0, b0), (a1, b1))):
            here = pl.ds(pl.multiple_of(h * size + t * step, step), step)
            o_ref[here, :] = a[...].astype(jnp.float32) + b[...].astype(jnp.float32)

    def own(h):
        return pl.BlockSpec((None, step, columns), lambda t, m: (m[0], (h * half + at) // step + t, 0))

    inside = pl.BlockSpec((step, columns), lambda t, m: (at // step + t, 0))
    return pl.pallas_call(
        kernel,
        grid_spec=pltpu.PrefetchScalarGridSpec(
            num_scalar_prefetch=1,
            grid=(size // step,),
            in_specs=[own(0), own(1), inside, inside],
            out_specs=whole_vmem,
        ),
        out_shape=pltpu.VMEM((2 * size, columns), jnp.float32),
        compiler_params=params_of(6 * MIB),
        cost_estimate=cost(2 * size * columns, 16 * size * columns),
        name="presum",
    )(me, parts, parts, *second)


def close(base, third, at, gradient, col_sums):
    rows, columns = gradient.shape
    half = rows // 2
    size = base.shape[0] // 2
    chunks = columns // LANES

    def kernel(base_ref, c0, c1, _, before_ref, g_ref, col_ref, row_ref, sums_ref):
        carry = tuple(jnp.zeros((8, LANES), jnp.float32) for _ in range(chunks))
        for h, c in enumerate((c0, c1)):

            def body(r, carry):
                here = pl.ds(pl.multiple_of(r * GROUP, GROUP), GROUP)
                there = pl.ds(pl.multiple_of(h * size + r * GROUP, GROUP), GROUP)
                kept = pl.ds(pl.multiple_of(h * half + at + r * GROUP, GROUP), GROUP)
                across = jnp.zeros((GROUP, LANES), jnp.float32)
                down = []
                for k in range(chunks):
                    lanes = slice(k * LANES, (k + 1) * LANES)
                    total = base_ref[there, lanes] + c[here, lanes].astype(jnp.float32)
                    g_ref[kept, lanes] = total.astype(g_ref.dtype)
                    square = total * total
                    across = across + square
                    down.append(carry[k] + square[:8] + square[8:])
                sums_ref[there, :] = across
                return tuple(down)

            carry = lax.fori_loop(0, size // GROUP, body, carry)
        for k in range(chunks):
            lanes = slice(k * LANES, (k + 1) * LANES)
            col_ref[:, lanes] = before_ref[:, lanes] + jnp.sum(carry[k], axis=0, keepdims=True)
        for q in range(2 * size // LANES):
            lanes = slice(q * LANES, (q + 1) * LANES)
            row_ref[:, lanes] = lane_sums(sums_ref[lanes, :])

    return pl.pallas_call(
        kernel,
        in_specs=[whole_vmem] * 3 + [anywhere, whole_vmem],
        out_specs=[whole_vmem] * 3,
        out_shape=[
            pltpu.VMEM((rows, columns), gradient.dtype),
            jax.ShapeDtypeStruct((1, columns), jnp.float32),
            jax.ShapeDtypeStruct((1, 2 * size), jnp.float32),
        ],
        input_output_aliases={3: 0},
        scratch_shapes=[pltpu.VMEM((2 * size, LANES), jnp.float32)],
        compiler_params=params_of(4 * MIB),
        cost_estimate=cost(10 * size * columns, 12 * size * columns),
        name="close",
    )(base, *third, gradient, col_sums)


def early(gradient, messages, row_moment, at, size):
    rows, columns = gradient.shape
    half = rows // 2
    chunks = columns // LANES
    n = len(messages)

    def kernel(g_ref, moment_ref, *refs):
        got, (new_ref, out_ref, root_ref, acc_ref) = refs[:n], refs[n:]
        total = tree([m[...] for m in got])
        for h in range(2):
            here = slice(h * size, (h + 1) * size)
            moment = moment_ref[:, h * half + at : h * half + at + size]
            new_ref[:, here] = DECAY * moment + (1.0 - DECAY) * (total[:, here] + FF * EPSILON) / FF
        root_ref[...] = lax.rsqrt(new_ref[...])
        acc_ref[...] = jnp.zeros_like(acc_ref)
        for h in range(2):

            def body(t, carry):
                lanes = root_ref[:, pl.ds(pl.multiple_of(h * size + t * TILE, TILE), TILE)]
                wide = jnp.broadcast_to(lanes, (LANES, TILE)).T
                for k in range(chunks):
                    at_lanes = slice(k * LANES, (k + 1) * LANES)
                    here = pl.ds(pl.multiple_of(h * half + at + t * TILE, TILE), TILE)
                    g = g_ref[here, at_lanes].astype(jnp.float32) * wide
                    square = g * g
                    acc_ref[:, at_lanes] += sum(square[i : i + 8] for i in range(8, TILE, 8)) + square[:8]
                return carry

            lax.fori_loop(0, size // TILE, body, 0)
        out_ref[...] = jnp.sum(acc_ref[...], axis=0, keepdims=True)

    return pl.pallas_call(
        kernel,
        in_specs=[whole_vmem] * (n + 2),
        out_specs=[whole_vmem] * 2,
        out_shape=[
            jax.ShapeDtypeStruct((1, 2 * size), jnp.float32),
            jax.ShapeDtypeStruct((1, columns), jnp.float32),
        ],
        scratch_shapes=[pltpu.VMEM((1, 2 * size), jnp.float32), pltpu.VMEM((8, columns), jnp.float32)],
        compiler_params=params_of(4 * MIB),
        cost_estimate=cost(8 * size * columns, 4 * size * columns),
        name="early",
    )(gradient, row_moment, *messages)


def power_of(params):
    rows, columns = params.shape
    steps = rows // TILE
    shares = min(SHARES, steps)
    each = steps // shares

    def kernel(p_ref, *refs):
        *kept, o_ref, sems = refs
        copies = []
        for t in range(steps):
            here, there = pl.ds(t * TILE, TILE), pl.ds(t % each * TILE, TILE)
            copies.append(pltpu.make_async_copy(p_ref.at[here], kept[t // each].at[there], sems.at[t]))
            copies[-1].start()
        total = jnp.zeros((8, LANES), jnp.float32)
        for t in range(steps):
            copies[t].wait()

            def body(r, total):
                here = pl.ds(pl.multiple_of(t % each * TILE + r * 8, 8), 8)
                for k in range(columns // LANES):
                    p = kept[t // each][here, k * LANES : (k + 1) * LANES]
                    total = total + p * p
                return total

            total = lax.fori_loop(0, TILE // 8, body, total)
        o_ref[...] = total

    *kept, power = pl.pallas_call(
        kernel,
        in_specs=[anywhere],
        out_specs=[whole_vmem] * (shares + 1),
        out_shape=[pltpu.VMEM((rows // shares, columns), jnp.float32)] * shares
        + [jax.ShapeDtypeStruct((8, LANES), jnp.float32)],
        scratch_shapes=[pltpu.SemaphoreType.DMA((steps,))],
        compiler_params=params_of(MIB),
        cost_estimate=cost(2 * rows * columns, 4 * rows * columns),
        name="param_power",
    )(in_hbm(params))
    return kept, power


def tree(values):
    while len(values) > 1:
        values = [a + b for a, b in zip(values[::2], values[1::2])]
    return values[0]


def weigh(gradient, col_sums, col_moment, row_pieces, early_sums, power, late):
    rows, columns = gradient.shape
    half = rows // 2
    chunks = columns // LANES
    n = len(col_sums)
    places = sorted(row_pieces)
    group = 4 * GROUP

    def kernel(g_ref, *refs):
        sums, refs = refs[:n], refs[n:]
        row_refs, refs = refs[: len(places)], refs[len(places) :]
        moment_ref, early_ref, power_ref, new_ref, root_ref, out_ref, wide_ref, acc_ref = refs
        total = tree([s[...] for s in sums]) + D * EPSILON
        new = DECAY * moment_ref[...] + (1.0 - DECAY) * total / D
        new_ref[...] = new
        root = lax.rsqrt(new)
        root_ref[...] = root
        wide_ref[...] = jnp.broadcast_to(root, wide_ref.shape)
        for at, row_ref in zip(places, row_refs):
            size = row_ref.shape[1] // 2
            for h in range(2):
                out_ref[:, h * late + at : h * late + at + size] = row_ref[:, h * size : (h + 1) * size]
        out_ref[:, 4 * late : 4 * late + LANES] = tree_lanes(early_ref[...] * (root * root), columns)
        out_ref[:, 4 * late + LANES :] = jnp.sum(power_ref[...], axis=0, keepdims=True)
        for h in range(2):

            def body(r, carry):
                here = pl.ds(pl.multiple_of(h * half + r * group, group), group)
                total = jnp.zeros((group, LANES), jnp.float32)
                for k in range(chunks):
                    lanes = slice(k * LANES, (k + 1) * LANES)
                    g = g_ref[here, lanes].astype(jnp.float32)
                    w = wide_ref[:, lanes]
                    g = jnp.concatenate([g[i : i + 8] * w for i in range(0, group, 8)], axis=0)
                    total = total + g * g
                acc_ref[pl.ds(pl.multiple_of(h * late + r * group, group), group), :] = total
                return carry

            lax.fori_loop(0, late // group, body, 0)
        for q in range(2 * late // LANES):
            lanes = slice(2 * late + q * LANES, 2 * late + (q + 1) * LANES)
            out_ref[:, lanes] = lane_sums(acc_ref[q * LANES : (q + 1) * LANES, :])

    return pl.pallas_call(
        kernel,
        in_specs=[whole_vmem] * (n + len(places) + 4),
        out_specs=[whole_vmem] * 3,
        out_shape=[
            jax.ShapeDtypeStruct((1, columns), jnp.float32),
            jax.ShapeDtypeStruct((1, columns), jnp.float32),
            jax.ShapeDtypeStruct((1, 4 * late + 2 * LANES), jnp.float32),
        ],
        scratch_shapes=[pltpu.VMEM((8, columns), jnp.float32), pltpu.VMEM((2 * late, LANES), jnp.float32)],
        compiler_params=params_of(4 * MIB),
        cost_estimate=cost(8 * late * columns, 4 * late * columns),
        name="weigh",
    )(gradient, *col_sums, *[row_pieces[at] for at in places], col_moment, early_sums, power)


def balance(messages, row_moment, new_early, late):
    rows = row_moment.shape[1]
    half = rows // 2
    first = half - late
    n = len(messages)

    def kernel(*refs):
        got, (moment_ref, early_ref, new_ref, root_ref, out_ref) = refs[:n], refs[n:]
        total = tree([m[...] for m in got])
        ratio = jnp.zeros((1, LANES), jnp.float32)
        for h in range(2):
            here = slice(h * half, h * half + late)
            there = slice(h * late, (h + 1) * late)
            new = DECAY * moment_ref[:, here] + (1.0 - DECAY) * (total[:, there] + FF * EPSILON) / FF
            new_ref[:, here] = new
            new_ref[:, h * half + late : (h + 1) * half] = early_ref[:, h * first : (h + 1) * first]
            ratio = ratio + tree_lanes(total[:, (2 + h) * late : (3 + h) * late] / new, late)
        root_ref[...] = lax.rsqrt(new_ref[...])
        out_ref[...] = jnp.zeros_like(out_ref)
        out_ref[0:1, :] = ratio + total[:, 4 * late : 4 * late + LANES]
        out_ref[1:2, :] = tree_lanes(new_ref[...], rows)
        out_ref[2:3, :] = total[:, 4 * late + LANES :]

    return pl.pallas_call(
        kernel,
        in_specs=[whole_vmem] * (n + 2),
        out_specs=[whole_vmem] * 3,
        out_shape=[
            jax.ShapeDtypeStruct((1, rows), jnp.float32),
            jax.ShapeDtypeStruct((1, rows), jnp.float32),
            jax.ShapeDtypeStruct((8, LANES), jnp.float32),
        ],
        compiler_params=params_of(4 * MIB),
        name="balance",
    )(*messages, row_moment, new_early)


def tree_lanes(x, rows):
    total = x[:, :LANES]
    for q in range(1, rows // LANES):
        total = total + x[:, q * LANES : (q + 1) * LANES]
    return total


def finish(gradient, params, row_root, col_root, stats):
    rows, columns = gradient.shape
    n = len(stats)
    shares = len(params)
    each = rows // shares // TILE
    group = 2 * GROUP

    def kernel(_, row_ref, col_ref, *refs):
        got, refs = refs[shares : shares + n], refs[shares + n :]
        g_ref, held, (new_ref, update_ref, scale_ref, sems) = refs[0], refs[1 : 1 + shares], refs[1 + shares :]
        total = jnp.sum(tree([s[...] for s in got]), axis=1, keepdims=True)
        mean = total[1:2] / D
        rms = jnp.sqrt(mean * total[0:1] / (D * FF))
        scale = jnp.sqrt(total[2:3] / (D * FF))
        factor = scale * jnp.sqrt(mean) / jnp.maximum(1.0, rms)
        scale_ref[...] = jnp.broadcast_to(col_ref[...] * factor, scale_ref.shape)

        def copies(q, t):
            here = pl.ds(pl.multiple_of((q * each + t) * TILE, TILE), TILE)
            there = pl.ds(pl.multiple_of(t * TILE, TILE), TILE)
            return (
                pltpu.make_async_copy(held[q].at[there], new_ref.at[here], sems.at[0, q * each + t]),
                pltpu.make_async_copy(g_ref.at[here], update_ref.at[here], sems.at[1, q * each + t]),
            )

        for q in range(shares):

            def block(t, carry):
                first = pl.multiple_of((q * each + t) * TILE, TILE)
                wide = jnp.broadcast_to(row_ref[:, pl.ds(first, TILE)], (LANES, TILE)).T
                for r in range(0, TILE, group):
                    here = pl.ds(pl.multiple_of(first + r, group), group)
                    there = pl.ds(pl.multiple_of(t * TILE + r, group), group)
                    root = wide[r : r + group, :]
                    for k in range(columns // LANES):
                        at = slice(k * LANES, (k + 1) * LANES)
                        g = g_ref[here, at].astype(jnp.float32)
                        s = scale_ref[:, at]
                        full = jnp.concatenate([g[i : i + 8] * s for i in range(0, group, 8)], axis=0) * root
                        g_ref[here, at] = full.astype(g_ref.dtype)
                        held[q][there, at] = held[q][there, at] - LEARN_RATE * full
                for copy in copies(q, t):
                    copy.start()
                return carry

            lax.fori_loop(0, each, block, 0)

        for q in range(shares):

            def drain(t, carry):
                for copy in copies(q, t):
                    copy.wait()
                return carry

            lax.fori_loop(0, each, drain, 0)

    out = pl.pallas_call(
        kernel,
        in_specs=[anywhere, whole_vmem, whole_vmem] + [anywhere] * shares + [whole_vmem] * n,
        out_specs=[whole_vmem] * (1 + shares) + [anywhere] * 2,
        out_shape=[pltpu.VMEM(x.shape, x.dtype) for x in (gradient, *params)]
        + [pltpu.HBM((rows, columns), jnp.float32), pltpu.HBM((rows, columns), jnp.bfloat16)],
        input_output_aliases={0: 0, **{3 + q: 1 + q for q in range(shares)}},
        scratch_shapes=[pltpu.VMEM((8, columns), jnp.float32), pltpu.SemaphoreType.DMA((2, rows // TILE))],
        compiler_params=params_of(4 * MIB),
        cost_estimate=cost(6 * rows * columns, 12 * rows * columns),
        name="finish",
    )(gradient, row_root, col_root, *params, *stats)
    return out[-2:]


def all_parts(value, axis, size):
    return [value] + [lax.ppermute(value, axis, pairs(size, k)) for k in range(1, size)]


def cut(half):
    units = half // TILE
    late = 2 if units > 3 else 1
    first = (units - late + 1) // 2 if units > 3 else units - late
    edges = [((units - first) * TILE, first * TILE)]
    if units - first > late:
        edges.append((late * TILE, (units - first - late) * TILE))
    return edges + [(0, late * TILE)]


def after(values, others):
    return lax.optimization_barrier((tuple(values), tuple(others)))[0]


def solution(mesh):
    across = mesh.shape["row"]
    along = mesh.shape["col"]

    def hop(values, lines):
        return [lax.ppermute(v, "dp", pairs(mesh.shape["dp"], n)) for v, n in zip(values, lines)]

    def on_device(grad_parts, params, row_moment, col_moment):
        parts = grad_parts[0]
        rows, columns = parts.shape[1:]
        half = rows // 2
        me = lax.axis_index("dp").astype(jnp.int32)[None]

        held = in_hbm(parts)
        pieces = cut(half)
        late = pieces[-1][1]
        rounds = []

        def send(values, lines):
            if len(rounds) > 1:
                values = after(values, rounds[-2])
            rounds.append(hop(values, lines))
            return rounds[-1]

        picked = grab(held, [(3, 0), (3, half)], TILE)
        (turn,) = after([me], picked)
        head = send(picked, NEAR)
        picked = pick(held, turn, [(3, TILE), (3, half + TILE)], half - TILE)
        (turn,) = after([me], picked)
        rest = send(picked, NEAR)
        second = send(pick(held, turn, [(NEAR[0], 0), (NEAR[1], half)], half), NEAR)

        third, done = [], []
        for at, size in pieces:
            if at:
                done = merge(held, me, after(rest, done), at, TILE, size)
            elif size == TILE:
                done = merge(held, me, after(head, done), 0, 0, size)
            else:
                done = merge(held, me, after(rest, done), 0, TILE, size, after(head, done))
            third.append(send(done, FAR))

        state, row_pieces = None, {}
        for i, ((at, size), came) in enumerate(zip(pieces[:-1], third)):
            if i + 2 == len(pieces):
                kept, power = power_of(after([params[0]], state[1:] if state else second)[0])
                base = presum(held, me, second, 0, late)
                came = after(came, [*kept, base])
            *state, row_pieces[at] = settle(held, me, second, came, at, size, state, 64)
        message = jnp.concatenate(
            [row_pieces[at][:, h * size : (h + 1) * size] for h in range(2) for at, size in sorted(pieces[:-1])], axis=1
        )
        new_early, early_sums = early(state[0], all_parts(message, "col", along), row_moment, late, half - late)
        gradient, col_sums, late_rows = close(base, third[-1], 0, *state)

        col_parts = all_parts(col_sums, "row", across)
        new_col, col_root, message = weigh(gradient, col_parts, col_moment, {0: late_rows}, early_sums, power, late)
        new_row, row_root, stats = balance(all_parts(message, "col", along), row_moment, new_early, late)
        new_params, update = finish(gradient, kept, row_root, col_root, all_parts(stats, "row", across))
        return new_params[None], update[None], new_row, new_col

    placed = (P("dp", None, "row", "col"), P("dp", "row", "col"), P("dp", "row"), P("dp", "col"))
    return jax.shard_map(
        on_device,
        mesh=mesh,
        in_specs=placed,
        out_specs=(P("dp", "row", "col"), P("dp", "row", "col"), P("dp", "row"), P("dp", "col")),
        check_vma=False,
    )
```

```python
import jax
import jax.numpy as jnp
from jax import lax
from jax.experimental import pallas as pl
from jax.experimental.pallas import tpu as pltpu
from jax.sharding import PartitionSpec as P

D = 4096
FF = 10240
EPSILON = 1e-30
DECAY = 0.8415106807538888
LEARN_RATE = 0.01
LANES = 128
TILE = 128
GROUP = 16
SHARES = 4
MIB = 1 << 20

NEAR = (1, 2)
FAR = (2, 1)

whole_vmem = pl.BlockSpec(memory_space=pltpu.VMEM)
anywhere = pl.BlockSpec(memory_space=pl.ANY)


def pairs(n, k):
    return [(i, i ^ k) for i in range(n)]


def in_hbm(x):
    return pltpu.with_memory_space_constraint(x, pltpu.HBM)


def cost(flops, bytes_accessed):
    return pl.CostEstimate(flops=flops, bytes_accessed=bytes_accessed, transcendentals=0)


def params_of(limit):
    return pltpu.CompilerParams(vmem_limit_bytes=limit)


def pick(parts, me, wants, size):
    columns = parts.shape[2]

    def kernel(me_ref, *refs):
        n = len(refs) // 2
        for a, b in zip(refs[:n], refs[n:]):
            b[...] = a[...]

    def spec(flip, start):
        return pl.BlockSpec((None, TILE, columns), lambda t, m: (m[0] ^ flip, start // TILE + t, 0))

    return pl.pallas_call(
        kernel,
        grid_spec=pltpu.PrefetchScalarGridSpec(
            num_scalar_prefetch=1,
            grid=(size // TILE,),
            in_specs=[spec(f, s) for f, s in wants],
            out_specs=[pl.BlockSpec((TILE, columns), lambda t, m: (t, 0)) for _ in wants],
        ),
        out_shape=[jax.ShapeDtypeStruct((size, columns), parts.dtype) for _ in wants],
        compiler_params=params_of(8 * MIB),
        cost_estimate=cost(0, 4 * len(wants) * size * columns),
        name="pick",
    )(me, *[parts] * len(wants))


def grab(parts, wants, size):
    columns = parts.shape[2]
    n = len(wants)

    def kernel(parts_ref, *refs):
        outs, sems = refs[:n], refs[n]
        me = lax.axis_index("dp")
        copies = []
        for i, (flip, start) in enumerate(wants):
            copies.append(pltpu.make_async_copy(parts_ref.at[me ^ flip, pl.ds(start, size)], outs[i], sems.at[i]))
            copies[-1].start()
        for copy in copies:
            copy.wait()

    return pl.pallas_call(
        kernel,
        in_specs=[anywhere],
        out_specs=[whole_vmem] * n,
        out_shape=[pltpu.VMEM((size, columns), parts.dtype)] * n,
        scratch_shapes=[pltpu.SemaphoreType.DMA((n,))],
        compiler_params=params_of(MIB),
        name="grab",
    )(parts)


def merge(parts, me, got, at, offset, size, lead=()):
    columns = parts.shape[2]
    half = parts.shape[1] // 2
    skip = 1 if lead else 0

    def add(o, a, b):
        o[...] = (a[...].astype(jnp.float32) + b[...].astype(jnp.float32)).astype(o.dtype)

    def kernel(me_ref, a0, a1, *refs):
        (o0, o1), refs = refs[-2:], refs[:-2]
        t = pl.program_id(0)

        @pl.when(t >= skip)
        def _():
            add(o0, a0, refs[-2])
            add(o1, a1, refs[-1])

        if lead:

            @pl.when(t == 0)
            def _():
                add(o0, a0, refs[0])
                add(o1, a1, refs[1])

    def own(h):
        return pl.BlockSpec((None, TILE, columns), lambda t, m: (m[0] ^ FAR[h], (h * half + at) // TILE + t, 0))

    first = at // TILE + skip - offset // TILE
    came = pl.BlockSpec((TILE, columns), lambda t, m: (first + jnp.maximum(t - skip, 0), 0))
    ahead = pl.BlockSpec((TILE, columns), lambda t, m: (0, 0))
    return pl.pallas_call(
        kernel,
        grid_spec=pltpu.PrefetchScalarGridSpec(
            num_scalar_prefetch=1,
            grid=(size // TILE,),
            in_specs=[own(0), own(1)] + [ahead] * len(lead) + [came, came],
            out_specs=[pl.BlockSpec((TILE, columns), lambda t, m: (t, 0))] * 2,
        ),
        out_shape=[jax.ShapeDtypeStruct((size, columns), parts.dtype)] * 2,
        compiler_params=params_of(12 * MIB),
        cost_estimate=cost(2 * size * columns, 12 * size * columns),
        name="merge",
    )(me, parts, parts, *lead, *got)


def lane_sums(x):
    return jnp.sum(x.T, axis=0, keepdims=True)


def settle(parts, me, second, third, at, size, state, step):
    rows, columns = parts.shape[1:]
    half = rows // 2
    chunks = columns // LANES
    steps = size // step

    def kernel(me_ref, a0, a1, b0, b1, c0, c1, *refs):
        before_ref = None
        if state is not None:
            before_ref, refs = refs[1], refs[2:]
        g_ref, col_ref, row_ref, sums_ref, carry_ref = refs
        t = pl.program_id(0)

        @pl.when(t == 0)
        def _():
            carry_ref[...] = jnp.zeros_like(carry_ref)

        for h, (a, b, c) in enumerate(((a0, b0, c0), (a1, b1, c1))):

            def body(r, carry):
                here = pl.ds(pl.multiple_of(r * GROUP, GROUP), GROUP)
                across = jnp.zeros((GROUP, LANES), jnp.float32)
                down = []
                for k in range(chunks):
                    lanes = slice(k * LANES, (k + 1) * LANES)
                    total = a[here, lanes].astype(jnp.float32) + b[here, lanes].astype(jnp.float32)
                    total = total + c[here, lanes].astype(jnp.float32)
                    first = pl.multiple_of(h * half + at + t * step + r * GROUP, GROUP)
                    g_ref[pl.ds(first, GROUP), lanes] = total.astype(g_ref.dtype)
                    square = total * total
                    across = across + square
                    down.append(carry[k] + square[:8] + square[8:])
                sums_ref[h, pl.ds(pl.multiple_of(t * step + r * GROUP, GROUP), GROUP), :] = across
                return tuple(down)

            carry = tuple(carry_ref[:, k * LANES : (k + 1) * LANES] for k in range(chunks))
            carry = lax.fori_loop(0, step // GROUP, body, carry)
            for k in range(chunks):
                carry_ref[:, k * LANES : (k + 1) * LANES] = carry[k]

        @pl.when(t == steps - 1)
        def _():
            for h in range(2):
                for q in range(size // LANES):
                    lanes = slice(q * LANES, (q + 1) * LANES)
                    row_ref[:, h * size + q * LANES : h * size + (q + 1) * LANES] = lane_sums(sums_ref[h, lanes, :])
            col_ref[...] = jnp.sum(carry_ref[...], axis=0, keepdims=True)
            if state is not None:
                col_ref[...] = col_ref[...] + before_ref[...]

    def own(h):
        return pl.BlockSpec((None, step, columns), lambda t, m: (m[0], (h * half + at) // step + t, 0))

    inside = pl.BlockSpec((step, columns), lambda t, m: (at // step + t, 0))
    piece = pl.BlockSpec((step, columns), lambda t, m: (t, 0))
    in_specs = [own(0), own(1), inside, inside, piece, piece]
    operands = [parts, parts, *second, *third]
    aliases = {}
    if state is not None:
        in_specs += [anywhere, whole_vmem]
        operands += state
        aliases = {7: 0}
    return pl.pallas_call(
        kernel,
        grid_spec=pltpu.PrefetchScalarGridSpec(
            num_scalar_prefetch=1,
            grid=(steps,),
            in_specs=in_specs,
            out_specs=[whole_vmem, whole_vmem, whole_vmem],
            scratch_shapes=[pltpu.VMEM((2, size, LANES), jnp.float32), pltpu.VMEM((8, columns), jnp.float32)],
        ),
        out_shape=[
            pltpu.VMEM((rows, columns), parts.dtype),
            jax.ShapeDtypeStruct((1, columns), jnp.float32),
            jax.ShapeDtypeStruct((1, 2 * size), jnp.float32),
        ],
        input_output_aliases=aliases,
        compiler_params=params_of(7 * MIB),
        cost_estimate=cost(12 * size * columns, 12 * size * columns),
        name="settle",
    )(me, *operands)


def presum(parts, me, second, at, size):
    columns = parts.shape[2]
    half = parts.shape[1] // 2
    step = min(64, size)

    def kernel(me_ref, a0, a1, b0, b1, o_ref):
        t = pl.program_id(0)
        for h, (a, b) in enumerate(((a0, b0), (a1, b1))):
            here = pl.ds(pl.multiple_of(h * size + t * step, step), step)
            o_ref[here, :] = a[...].astype(jnp.float32) + b[...].astype(jnp.float32)

    def own(h):
        return pl.BlockSpec((None, step, columns), lambda t, m: (m[0], (h * half + at) // step + t, 0))

    inside = pl.BlockSpec((step, columns), lambda t, m: (at // step + t, 0))
    return pl.pallas_call(
        kernel,
        grid_spec=pltpu.PrefetchScalarGridSpec(
            num_scalar_prefetch=1,
            grid=(size // step,),
            in_specs=[own(0), own(1), inside, inside],
            out_specs=whole_vmem,
        ),
        out_shape=pltpu.VMEM((2 * size, columns), jnp.float32),
        compiler_params=params_of(6 * MIB),
        cost_estimate=cost(2 * size * columns, 16 * size * columns),
        name="presum",
    )(me, parts, parts, *second)


def close(base, third, at, gradient, col_sums):
    rows, columns = gradient.shape
    half = rows // 2
    size = base.shape[0] // 2
    chunks = columns // LANES

    def kernel(base_ref, c0, c1, _, before_ref, g_ref, col_ref, row_ref, sums_ref):
        carry = tuple(jnp.zeros((8, LANES), jnp.float32) for _ in range(chunks))
        for h, c in enumerate((c0, c1)):

            def body(r, carry):
                here = pl.ds(pl.multiple_of(r * GROUP, GROUP), GROUP)
                there = pl.ds(pl.multiple_of(h * size + r * GROUP, GROUP), GROUP)
                kept = pl.ds(pl.multiple_of(h * half + at + r * GROUP, GROUP), GROUP)
                across = jnp.zeros((GROUP, LANES), jnp.float32)
                down = []
                for k in range(chunks):
                    lanes = slice(k * LANES, (k + 1) * LANES)
                    total = base_ref[there, lanes] + c[here, lanes].astype(jnp.float32)
                    g_ref[kept, lanes] = total.astype(g_ref.dtype)
                    square = total * total
                    across = across + square
                    down.append(carry[k] + square[:8] + square[8:])
                sums_ref[there, :] = across
                return tuple(down)

            carry = lax.fori_loop(0, size // GROUP, body, carry)
        for k in range(chunks):
            lanes = slice(k * LANES, (k + 1) * LANES)
            col_ref[:, lanes] = before_ref[:, lanes] + jnp.sum(carry[k], axis=0, keepdims=True)
        for q in range(2 * size // LANES):
            lanes = slice(q * LANES, (q + 1) * LANES)
            row_ref[:, lanes] = lane_sums(sums_ref[lanes, :])

    return pl.pallas_call(
        kernel,
        in_specs=[whole_vmem] * 3 + [anywhere, whole_vmem],
        out_specs=[whole_vmem] * 3,
        out_shape=[
            pltpu.VMEM((rows, columns), gradient.dtype),
            jax.ShapeDtypeStruct((1, columns), jnp.float32),
            jax.ShapeDtypeStruct((1, 2 * size), jnp.float32),
        ],
        input_output_aliases={3: 0},
        scratch_shapes=[pltpu.VMEM((2 * size, LANES), jnp.float32)],
        compiler_params=params_of(4 * MIB),
        cost_estimate=cost(10 * size * columns, 12 * size * columns),
        name="close",
    )(base, *third, gradient, col_sums)


def early(gradient, messages, row_moment, at, size):
    rows, columns = gradient.shape
    half = rows // 2
    chunks = columns // LANES
    n = len(messages)

    def kernel(g_ref, moment_ref, *refs):
        got, (new_ref, out_ref, root_ref, acc_ref) = refs[:n], refs[n:]
        total = tree([m[...] for m in got])
        for h in range(2):
            here = slice(h * size, (h + 1) * size)
            moment = moment_ref[:, h * half + at : h * half + at + size]
            new_ref[:, here] = DECAY * moment + (1.0 - DECAY) * (total[:, here] + FF * EPSILON) / FF
        root_ref[...] = lax.rsqrt(new_ref[...])
        acc_ref[...] = jnp.zeros_like(acc_ref)
        for h in range(2):

            def body(t, carry):
                lanes = root_ref[:, pl.ds(pl.multiple_of(h * size + t * TILE, TILE), TILE)]
                wide = jnp.broadcast_to(lanes, (LANES, TILE)).T
                for k in range(chunks):
                    at_lanes = slice(k * LANES, (k + 1) * LANES)
                    here = pl.ds(pl.multiple_of(h * half + at + t * TILE, TILE), TILE)
                    g = g_ref[here, at_lanes].astype(jnp.float32) * wide
                    square = g * g
                    acc_ref[:, at_lanes] += sum(square[i : i + 8] for i in range(8, TILE, 8)) + square[:8]
                return carry

            lax.fori_loop(0, size // TILE, body, 0)
        out_ref[...] = jnp.sum(acc_ref[...], axis=0, keepdims=True)

    return pl.pallas_call(
        kernel,
        in_specs=[whole_vmem] * (n + 2),
        out_specs=[whole_vmem] * 2,
        out_shape=[
            jax.ShapeDtypeStruct((1, 2 * size), jnp.float32),
            jax.ShapeDtypeStruct((1, columns), jnp.float32),
        ],
        scratch_shapes=[pltpu.VMEM((1, 2 * size), jnp.float32), pltpu.VMEM((8, columns), jnp.float32)],
        compiler_params=params_of(4 * MIB),
        cost_estimate=cost(8 * size * columns, 4 * size * columns),
        name="early",
    )(gradient, row_moment, *messages)


def power_of(params):
    rows, columns = params.shape
    steps = rows // TILE
    shares = min(SHARES, steps)
    each = steps // shares

    def kernel(p_ref, *refs):
        *kept, o_ref, sems = refs
        copies = []
        for t in range(steps):
            here, there = pl.ds(t * TILE, TILE), pl.ds(t % each * TILE, TILE)
            copies.append(pltpu.make_async_copy(p_ref.at[here], kept[t // each].at[there], sems.at[t]))
            copies[-1].start()
        total = jnp.zeros((8, LANES), jnp.float32)
        for t in range(steps):
            copies[t].wait()

            def body(r, total):
                here = pl.ds(pl.multiple_of(t % each * TILE + r * 8, 8), 8)
                for k in range(columns // LANES):
                    p = kept[t // each][here, k * LANES : (k + 1) * LANES]
                    total = total + p * p
                return total

            total = lax.fori_loop(0, TILE // 8, body, total)
        o_ref[...] = total

    *kept, power = pl.pallas_call(
        kernel,
        in_specs=[anywhere],
        out_specs=[whole_vmem] * (shares + 1),
        out_shape=[pltpu.VMEM((rows // shares, columns), jnp.float32)] * shares
        + [jax.ShapeDtypeStruct((8, LANES), jnp.float32)],
        scratch_shapes=[pltpu.SemaphoreType.DMA((steps,))],
        compiler_params=params_of(MIB),
        cost_estimate=cost(2 * rows * columns, 4 * rows * columns),
        name="param_power",
    )(in_hbm(params))
    return kept, power


def tree(values):
    while len(values) > 1:
        values = [a + b for a, b in zip(values[::2], values[1::2])]
    return values[0]


def weigh(gradient, col_sums, col_moment, row_pieces, early_sums, power, late):
    rows, columns = gradient.shape
    half = rows // 2
    chunks = columns // LANES
    n = len(col_sums)
    places = sorted(row_pieces)
    group = 4 * GROUP

    def kernel(g_ref, *refs):
        sums, refs = refs[:n], refs[n:]
        row_refs, refs = refs[: len(places)], refs[len(places) :]
        moment_ref, early_ref, power_ref, new_ref, root_ref, out_ref, wide_ref, acc_ref = refs
        total = tree([s[...] for s in sums]) + D * EPSILON
        new = DECAY * moment_ref[...] + (1.0 - DECAY) * total / D
        new_ref[...] = new
        root = lax.rsqrt(new)
        root_ref[...] = root
        wide_ref[...] = jnp.broadcast_to(root, wide_ref.shape)
        for at, row_ref in zip(places, row_refs):
            size = row_ref.shape[1] // 2
            for h in range(2):
                out_ref[:, h * late + at : h * late + at + size] = row_ref[:, h * size : (h + 1) * size]
        out_ref[:, 4 * late : 4 * late + LANES] = tree_lanes(early_ref[...] * (root * root), columns)
        out_ref[:, 4 * late + LANES :] = jnp.sum(power_ref[...], axis=0, keepdims=True)
        for h in range(2):

            def body(r, carry):
                here = pl.ds(pl.multiple_of(h * half + r * group, group), group)
                total = jnp.zeros((group, LANES), jnp.float32)
                for k in range(chunks):
                    lanes = slice(k * LANES, (k + 1) * LANES)
                    g = g_ref[here, lanes].astype(jnp.float32)
                    w = wide_ref[:, lanes]
                    g = jnp.concatenate([g[i : i + 8] * w for i in range(0, group, 8)], axis=0)
                    total = total + g * g
                acc_ref[pl.ds(pl.multiple_of(h * late + r * group, group), group), :] = total
                return carry

            lax.fori_loop(0, late // group, body, 0)
        for q in range(2 * late // LANES):
            lanes = slice(2 * late + q * LANES, 2 * late + (q + 1) * LANES)
            out_ref[:, lanes] = lane_sums(acc_ref[q * LANES : (q + 1) * LANES, :])

    return pl.pallas_call(
        kernel,
        in_specs=[whole_vmem] * (n + len(places) + 4),
        out_specs=[whole_vmem] * 3,
        out_shape=[
            pltpu.VMEM((1, columns), jnp.float32),
            pltpu.VMEM((1, columns), jnp.float32),
            pltpu.VMEM((1, 4 * late + 2 * LANES), jnp.float32),
        ],
        scratch_shapes=[pltpu.VMEM((8, columns), jnp.float32), pltpu.VMEM((2 * late, LANES), jnp.float32)],
        compiler_params=params_of(4 * MIB),
        cost_estimate=cost(8 * late * columns, 4 * late * columns),
        name="weigh",
    )(gradient, *col_sums, *[row_pieces[at] for at in places], col_moment, early_sums, power)


def balance(messages, row_moment, new_early, late):
    rows = row_moment.shape[1]
    half = rows // 2
    first = half - late
    n = len(messages)

    def kernel(*refs):
        got, (moment_ref, early_ref, new_ref, root_ref, out_ref) = refs[:n], refs[n:]
        total = tree([m[...] for m in got])
        ratio = jnp.zeros((1, LANES), jnp.float32)
        for h in range(2):
            here = slice(h * half, h * half + late)
            there = slice(h * late, (h + 1) * late)
            new = DECAY * moment_ref[:, here] + (1.0 - DECAY) * (total[:, there] + FF * EPSILON) / FF
            new_ref[:, here] = new
            new_ref[:, h * half + late : (h + 1) * half] = early_ref[:, h * first : (h + 1) * first]
            ratio = ratio + tree_lanes(total[:, (2 + h) * late : (3 + h) * late] / new, late)
        root_ref[...] = lax.rsqrt(new_ref[...])
        out_ref[...] = jnp.zeros_like(out_ref)
        out_ref[0:1, :] = ratio + total[:, 4 * late : 4 * late + LANES]
        out_ref[1:2, :] = tree_lanes(new_ref[...], rows)
        out_ref[2:3, :] = total[:, 4 * late + LANES :]

    return pl.pallas_call(
        kernel,
        in_specs=[whole_vmem] * (n + 2),
        out_specs=[whole_vmem] * 3,
        out_shape=[
            pltpu.VMEM((1, rows), jnp.float32),
            pltpu.VMEM((1, rows), jnp.float32),
            pltpu.VMEM((8, LANES), jnp.float32),
        ],
        compiler_params=params_of(4 * MIB),
        name="balance",
    )(*messages, row_moment, new_early)


def tree_lanes(x, rows):
    total = x[:, :LANES]
    for q in range(1, rows // LANES):
        total = total + x[:, q * LANES : (q + 1) * LANES]
    return total


def finish(gradient, params, row_root, col_root, stats):
    rows, columns = gradient.shape
    n = len(stats)
    shares = len(params)
    each = rows // shares // TILE
    group = 2 * GROUP

    def kernel(_, row_ref, col_ref, *refs):
        got, refs = refs[shares : shares + n], refs[shares + n :]
        g_ref, held, (new_ref, update_ref, scale_ref, sems, first_sems) = refs[0], refs[1 : 1 + shares], refs[1 + shares :]
        total = jnp.sum(tree([s[...] for s in got]), axis=1, keepdims=True)
        mean = total[1:2] / D
        rms = jnp.sqrt(mean * total[0:1] / (D * FF))
        scale = jnp.sqrt(total[2:3] / (D * FF))
        factor = scale * jnp.sqrt(mean) / jnp.maximum(1.0, rms)
        scale_ref[...] = jnp.broadcast_to(col_ref[...] * factor, scale_ref.shape)

        def copies(q, t):
            here = pl.ds(pl.multiple_of((q * each + t) * TILE, TILE), TILE)
            there = pl.ds(pl.multiple_of(t * TILE, TILE), TILE)
            return (
                pltpu.make_async_copy(held[q].at[there], new_ref.at[here], sems.at[0, q * each + t]),
                pltpu.make_async_copy(g_ref.at[here], update_ref.at[here], sems.at[1, q * each + t]),
            )

        def opening(r):
            here = pl.ds(r * group, group)
            return (
                pltpu.make_async_copy(held[0].at[here], new_ref.at[here], first_sems.at[0, r]),
                pltpu.make_async_copy(g_ref.at[here], update_ref.at[here], first_sems.at[1, r]),
            )

        def rows_of(q, t, wide, r):
            here = pl.ds(pl.multiple_of((q * each + t) * TILE + r * group, group), group)
            there = pl.ds(pl.multiple_of(t * TILE + r * group, group), group)
            root = wide[r * group : (r + 1) * group, :]
            for k in range(columns // LANES):
                at = slice(k * LANES, (k + 1) * LANES)
                g = g_ref[here, at].astype(jnp.float32)
                s = scale_ref[:, at]
                full = jnp.concatenate([g[i : i + 8] * s for i in range(0, group, 8)], axis=0) * root
                g_ref[here, at] = full.astype(g_ref.dtype)
                held[q][there, at] = held[q][there, at] - LEARN_RATE * full

        def widen(q, t):
            lanes = row_ref[:, pl.ds(pl.multiple_of((q * each + t) * TILE, TILE), TILE)]
            return jnp.broadcast_to(lanes, (LANES, TILE)).T

        wide = widen(0, 0)
        for r in range(TILE // group):
            rows_of(0, 0, wide, r)
            for copy in opening(r):
                copy.start()

        for q in range(shares):

            def block(t, carry):
                wide = widen(q, t)
                for r in range(TILE // group):
                    rows_of(q, t, wide, r)
                for copy in copies(q, t):
                    copy.start()
                return carry

            lax.fori_loop(0 if q else 1, each, block, 0)

        for r in range(TILE // group):
            for copy in opening(r):
                copy.wait()
        for q in range(shares):

            def drain(t, carry):
                for copy in copies(q, t):
                    copy.wait()
                return carry

            lax.fori_loop(0 if q else 1, each, drain, 0)

    out = pl.pallas_call(
        kernel,
        in_specs=[anywhere, whole_vmem, whole_vmem] + [anywhere] * shares + [whole_vmem] * n,
        out_specs=[whole_vmem] * (1 + shares) + [anywhere] * 2,
        out_shape=[pltpu.VMEM(x.shape, x.dtype) for x in (gradient, *params)]
        + [pltpu.HBM((rows, columns), jnp.float32), pltpu.HBM((rows, columns), jnp.bfloat16)],
        input_output_aliases={0: 0, **{3 + q: 1 + q for q in range(shares)}},
        scratch_shapes=[
            pltpu.VMEM((8, columns), jnp.float32),
            pltpu.SemaphoreType.DMA((2, rows // TILE)),
            pltpu.SemaphoreType.DMA((2, TILE // group)),
        ],
        compiler_params=params_of(4 * MIB),
        cost_estimate=cost(6 * rows * columns, 12 * rows * columns),
        name="finish",
    )(gradient, row_root, col_root, *params, *stats)
    return out[-2:]


def all_parts(value, axis, size):
    return [value] + [lax.ppermute(value, axis, pairs(size, k)) for k in range(1, size)]


def cut(half):
    units = half // TILE
    late = 2 if units > 3 else 1
    first = (units - late + 1) // 2 if units > 3 else units - late
    edges = [((units - first) * TILE, first * TILE)]
    if units - first > late:
        edges.append((late * TILE, (units - first - late) * TILE))
    return edges + [(0, late * TILE)]


def after(values, others):
    return lax.optimization_barrier((tuple(values), tuple(others)))[0]


def solution(mesh):
    across = mesh.shape["row"]
    along = mesh.shape["col"]

    def hop(values, lines):
        return [lax.ppermute(v, "dp", pairs(mesh.shape["dp"], n)) for v, n in zip(values, lines)]

    def on_device(grad_parts, params, row_moment, col_moment):
        parts = grad_parts[0]
        rows, columns = parts.shape[1:]
        half = rows // 2
        me = lax.axis_index("dp").astype(jnp.int32)[None]

        held = in_hbm(parts)
        pieces = cut(half)
        late = pieces[-1][1]
        rounds = []

        def send(values, lines):
            if len(rounds) > 1:
                values = after(values, rounds[-2])
            rounds.append(hop(values, lines))
            return rounds[-1]

        picked = grab(held, [(3, 0), (3, half)], TILE)
        (turn,) = after([me], picked)
        head = send(picked, NEAR)
        picked = pick(held, turn, [(3, TILE), (3, half + TILE)], half - TILE)
        (turn,) = after([me], picked)
        rest = send(picked, NEAR)
        second = send(pick(held, turn, [(NEAR[0], 0), (NEAR[1], half)], half), NEAR)

        third, done = [], []
        for at, size in pieces:
            if at:
                done = merge(held, me, after(rest, done), at, TILE, size)
            elif size == TILE:
                done = merge(held, me, after(head, done), 0, 0, size)
            else:
                done = merge(held, me, after(rest, done), 0, TILE, size, after(head, done))
            third.append(send(done, FAR))

        state, row_pieces = None, {}
        for i, ((at, size), came) in enumerate(zip(pieces[:-1], third)):
            if i + 2 == len(pieces):
                kept, power = power_of(after([params[0]], state[1:] if state else second)[0])
                base = presum(held, me, second, 0, late)
                came = after(came, [*kept, base])
            *state, row_pieces[at] = settle(held, me, second, came, at, size, state, 64)
        message = jnp.concatenate(
            [row_pieces[at][:, h * size : (h + 1) * size] for h in range(2) for at, size in sorted(pieces[:-1])], axis=1
        )
        new_early, early_sums = early(state[0], all_parts(message, "col", along), row_moment, late, half - late)
        gradient, col_sums, late_rows = close(base, third[-1], 0, *state)

        col_parts = all_parts(col_sums, "row", across)
        new_col, col_root, message = weigh(gradient, col_parts, col_moment, {0: late_rows}, early_sums, power, late)
        new_row, row_root, stats = balance(all_parts(message, "col", along), row_moment, new_early, late)
        new_params, update = finish(gradient, kept, row_root, col_root, all_parts(stats, "row", across))
        return new_params[None], update[None], new_row, new_col

    placed = (P("dp", None, "row", "col"), P("dp", "row", "col"), P("dp", "row"), P("dp", "col"))
    return jax.shard_map(
        on_device,
        mesh=mesh,
        in_specs=placed,
        out_specs=(P("dp", "row", "col"), P("dp", "row", "col"), P("dp", "row"), P("dp", "col")),
        check_vma=False,
    )
```

```python
import jax
import jax.numpy as jnp
from jax import lax
from jax.experimental import pallas as pl
from jax.experimental.pallas import tpu as pltpu
from jax.sharding import PartitionSpec as P

D = 4096
FF = 10240
EPSILON = 1e-30
DECAY = 0.8415106807538888
LEARN_RATE = 0.01
LANES = 128
TILE = 128
GROUP = 16
SHARES = 4
MIB = 1 << 20

NEAR = (1, 2)
FAR = (2, 1)

whole_vmem = pl.BlockSpec(memory_space=pltpu.VMEM)
anywhere = pl.BlockSpec(memory_space=pl.ANY)


def pairs(n, k):
    return [(i, i ^ k) for i in range(n)]


def in_hbm(x):
    return pltpu.with_memory_space_constraint(x, pltpu.HBM)


def cost(flops, bytes_accessed):
    return pl.CostEstimate(flops=flops, bytes_accessed=bytes_accessed, transcendentals=0)


def params_of(limit):
    return pltpu.CompilerParams(vmem_limit_bytes=limit)


def pick(parts, me, wants, size):
    columns = parts.shape[2]

    def kernel(me_ref, *refs):
        n = len(refs) // 2
        for a, b in zip(refs[:n], refs[n:]):
            b[...] = a[...]

    def spec(flip, start):
        return pl.BlockSpec((None, TILE, columns), lambda t, m: (m[0] ^ flip, start // TILE + t, 0))

    return pl.pallas_call(
        kernel,
        grid_spec=pltpu.PrefetchScalarGridSpec(
            num_scalar_prefetch=1,
            grid=(size // TILE,),
            in_specs=[spec(f, s) for f, s in wants],
            out_specs=[pl.BlockSpec((TILE, columns), lambda t, m: (t, 0)) for _ in wants],
        ),
        out_shape=[jax.ShapeDtypeStruct((size, columns), parts.dtype) for _ in wants],
        compiler_params=params_of(8 * MIB),
        cost_estimate=cost(0, 4 * len(wants) * size * columns),
        name="pick",
    )(me, *[parts] * len(wants))


def grab(parts, wants, size):
    columns = parts.shape[2]
    n = len(wants)

    def kernel(parts_ref, *refs):
        outs, sems = refs[:n], refs[n]
        me = lax.axis_index("dp")
        copies = []
        for i, (flip, start) in enumerate(wants):
            copies.append(pltpu.make_async_copy(parts_ref.at[me ^ flip, pl.ds(start, size)], outs[i], sems.at[i]))
            copies[-1].start()
        for copy in copies:
            copy.wait()

    return pl.pallas_call(
        kernel,
        in_specs=[anywhere],
        out_specs=[whole_vmem] * n,
        out_shape=[pltpu.VMEM((size, columns), parts.dtype)] * n,
        scratch_shapes=[pltpu.SemaphoreType.DMA((n,))],
        compiler_params=params_of(MIB),
        name="grab",
    )(parts)


def merge(parts, me, got, at, offset, size, lead=()):
    columns = parts.shape[2]
    half = parts.shape[1] // 2
    skip = 1 if lead else 0

    def add(o, a, b):
        o[...] = (a[...].astype(jnp.float32) + b[...].astype(jnp.float32)).astype(o.dtype)

    def kernel(me_ref, a0, a1, *refs):
        (o0, o1), refs = refs[-2:], refs[:-2]
        t = pl.program_id(0)

        @pl.when(t >= skip)
        def _():
            add(o0, a0, refs[-2])
            add(o1, a1, refs[-1])

        if lead:

            @pl.when(t == 0)
            def _():
                add(o0, a0, refs[0])
                add(o1, a1, refs[1])

    def own(h):
        return pl.BlockSpec((None, TILE, columns), lambda t, m: (m[0] ^ FAR[h], (h * half + at) // TILE + t, 0))

    first = at // TILE + skip - offset // TILE
    came = pl.BlockSpec((TILE, columns), lambda t, m: (first + jnp.maximum(t - skip, 0), 0))
    ahead = pl.BlockSpec((TILE, columns), lambda t, m: (0, 0))
    return pl.pallas_call(
        kernel,
        grid_spec=pltpu.PrefetchScalarGridSpec(
            num_scalar_prefetch=1,
            grid=(size // TILE,),
            in_specs=[own(0), own(1)] + [ahead] * len(lead) + [came, came],
            out_specs=[pl.BlockSpec((TILE, columns), lambda t, m: (t, 0))] * 2,
        ),
        out_shape=[jax.ShapeDtypeStruct((size, columns), parts.dtype)] * 2,
        compiler_params=params_of(12 * MIB),
        cost_estimate=cost(2 * size * columns, 12 * size * columns),
        name="merge",
    )(me, parts, parts, *lead, *got)


def lane_sums(x):
    return jnp.sum(x.T, axis=0, keepdims=True)


def settle(parts, me, second, third, at, size, state, step):
    rows, columns = parts.shape[1:]
    half = rows // 2
    chunks = columns // LANES
    steps = size // step

    def kernel(me_ref, a0, a1, b0, b1, c0, c1, *refs):
        before_ref = None
        if state is not None:
            before_ref, refs = refs[1], refs[2:]
        g_ref, col_ref, row_ref, sums_ref, carry_ref = refs
        t = pl.program_id(0)

        @pl.when(t == 0)
        def _():
            carry_ref[...] = jnp.zeros_like(carry_ref)

        for h, (a, b, c) in enumerate(((a0, b0, c0), (a1, b1, c1))):

            def body(r, carry):
                here = pl.ds(pl.multiple_of(r * GROUP, GROUP), GROUP)
                across = jnp.zeros((GROUP, LANES), jnp.float32)
                down = []
                for k in range(chunks):
                    lanes = slice(k * LANES, (k + 1) * LANES)
                    total = a[here, lanes].astype(jnp.float32) + b[here, lanes].astype(jnp.float32)
                    total = total + c[here, lanes].astype(jnp.float32)
                    first = pl.multiple_of(h * half + at + t * step + r * GROUP, GROUP)
                    g_ref[pl.ds(first, GROUP), lanes] = total.astype(g_ref.dtype)
                    square = total * total
                    across = across + square
                    down.append(carry[k] + square[:8] + square[8:])
                sums_ref[h, pl.ds(pl.multiple_of(t * step + r * GROUP, GROUP), GROUP), :] = across
                return tuple(down)

            carry = tuple(carry_ref[:, k * LANES : (k + 1) * LANES] for k in range(chunks))
            carry = lax.fori_loop(0, step // GROUP, body, carry)
            for k in range(chunks):
                carry_ref[:, k * LANES : (k + 1) * LANES] = carry[k]

        @pl.when(t == steps - 1)
        def _():
            for h in range(2):
                for q in range(size // LANES):
                    lanes = slice(q * LANES, (q + 1) * LANES)
                    row_ref[:, h * size + q * LANES : h * size + (q + 1) * LANES] = lane_sums(sums_ref[h, lanes, :])
            col_ref[...] = jnp.sum(carry_ref[...], axis=0, keepdims=True)
            if state is not None:
                col_ref[...] = col_ref[...] + before_ref[...]

    def own(h):
        return pl.BlockSpec((None, step, columns), lambda t, m: (m[0], (h * half + at) // step + t, 0))

    inside = pl.BlockSpec((step, columns), lambda t, m: (at // step + t, 0))
    piece = pl.BlockSpec((step, columns), lambda t, m: (t, 0))
    in_specs = [own(0), own(1), inside, inside, piece, piece]
    operands = [parts, parts, *second, *third]
    aliases = {}
    if state is not None:
        in_specs += [anywhere, whole_vmem]
        operands += state
        aliases = {7: 0}
    return pl.pallas_call(
        kernel,
        grid_spec=pltpu.PrefetchScalarGridSpec(
            num_scalar_prefetch=1,
            grid=(steps,),
            in_specs=in_specs,
            out_specs=[whole_vmem, whole_vmem, whole_vmem],
            scratch_shapes=[pltpu.VMEM((2, size, LANES), jnp.float32), pltpu.VMEM((8, columns), jnp.float32)],
        ),
        out_shape=[
            pltpu.VMEM((rows, columns), parts.dtype),
            jax.ShapeDtypeStruct((1, columns), jnp.float32),
            jax.ShapeDtypeStruct((1, 2 * size), jnp.float32),
        ],
        input_output_aliases=aliases,
        compiler_params=params_of(7 * MIB),
        cost_estimate=cost(12 * size * columns, 12 * size * columns),
        name="settle",
    )(me, *operands)


def presum(parts, me, second, at, size):
    columns = parts.shape[2]
    half = parts.shape[1] // 2
    step = min(64, size)

    def kernel(me_ref, a0, a1, b0, b1, o_ref):
        t = pl.program_id(0)
        for h, (a, b) in enumerate(((a0, b0), (a1, b1))):
            here = pl.ds(pl.multiple_of(h * size + t * step, step), step)
            o_ref[here, :] = a[...].astype(jnp.float32) + b[...].astype(jnp.float32)

    def own(h):
        return pl.BlockSpec((None, step, columns), lambda t, m: (m[0], (h * half + at) // step + t, 0))

    inside = pl.BlockSpec((step, columns), lambda t, m: (at // step + t, 0))
    return pl.pallas_call(
        kernel,
        grid_spec=pltpu.PrefetchScalarGridSpec(
            num_scalar_prefetch=1,
            grid=(size // step,),
            in_specs=[own(0), own(1), inside, inside],
            out_specs=whole_vmem,
        ),
        out_shape=pltpu.VMEM((2 * size, columns), jnp.float32),
        compiler_params=params_of(6 * MIB),
        cost_estimate=cost(2 * size * columns, 16 * size * columns),
        name="presum",
    )(me, parts, parts, *second)


def close(base, came, h, gradient, col_sums):
    rows, columns = gradient.shape
    half = rows // 2
    size = came.shape[0]
    chunks = columns // LANES

    def kernel(base_ref, came_ref, _, before_ref, g_ref, col_ref, row_ref, sums_ref):
        def body(r, carry):
            here = pl.ds(pl.multiple_of(r * GROUP, GROUP), GROUP)
            there = pl.ds(pl.multiple_of(h * size + r * GROUP, GROUP), GROUP)
            kept = pl.ds(pl.multiple_of(h * half + r * GROUP, GROUP), GROUP)
            across = jnp.zeros((GROUP, LANES), jnp.float32)
            down = []
            for k in range(chunks):
                lanes = slice(k * LANES, (k + 1) * LANES)
                total = base_ref[there, lanes] + came_ref[here, lanes].astype(jnp.float32)
                g_ref[kept, lanes] = total.astype(g_ref.dtype)
                square = total * total
                across = across + square
                down.append(carry[k] + square[:8] + square[8:])
            sums_ref[here, :] = across
            return tuple(down)

        carry = tuple(jnp.zeros((8, LANES), jnp.float32) for _ in range(chunks))
        carry = lax.fori_loop(0, size // GROUP, body, carry)
        for k in range(chunks):
            lanes = slice(k * LANES, (k + 1) * LANES)
            col_ref[:, lanes] = before_ref[:, lanes] + jnp.sum(carry[k], axis=0, keepdims=True)
        for q in range(size // LANES):
            lanes = slice(q * LANES, (q + 1) * LANES)
            row_ref[:, lanes] = lane_sums(sums_ref[lanes, :])

    return pl.pallas_call(
        kernel,
        in_specs=[whole_vmem] * 2 + [anywhere, whole_vmem],
        out_specs=[whole_vmem] * 3,
        out_shape=[
            pltpu.VMEM((rows, columns), gradient.dtype),
            pltpu.VMEM((1, columns), jnp.float32),
            pltpu.VMEM((1, size), jnp.float32),
        ],
        input_output_aliases={2: 0},
        scratch_shapes=[pltpu.VMEM((size, LANES), jnp.float32)],
        compiler_params=params_of(4 * MIB),
        cost_estimate=cost(5 * size * columns, 6 * size * columns),
        name="close",
    )(base, came, gradient, col_sums)


def early(gradient, messages, row_moment, at, size):
    rows, columns = gradient.shape
    half = rows // 2
    chunks = columns // LANES
    n = len(messages)

    def kernel(g_ref, moment_ref, *refs):
        got, (new_ref, out_ref, root_ref, acc_ref) = refs[:n], refs[n:]
        total = tree([m[...] for m in got])
        for h in range(2):
            here = slice(h * size, (h + 1) * size)
            moment = moment_ref[:, h * half + at : h * half + at + size]
            new_ref[:, here] = DECAY * moment + (1.0 - DECAY) * (total[:, here] + FF * EPSILON) / FF
        root_ref[...] = lax.rsqrt(new_ref[...])
        acc_ref[...] = jnp.zeros_like(acc_ref)
        for h in range(2):

            def body(t, carry):
                lanes = root_ref[:, pl.ds(pl.multiple_of(h * size + t * TILE, TILE), TILE)]
                wide = jnp.broadcast_to(lanes, (LANES, TILE)).T
                for k in range(chunks):
                    at_lanes = slice(k * LANES, (k + 1) * LANES)
                    here = pl.ds(pl.multiple_of(h * half + at + t * TILE, TILE), TILE)
                    g = g_ref[here, at_lanes].astype(jnp.float32) * wide
                    square = g * g
                    acc_ref[:, at_lanes] += sum(square[i : i + 8] for i in range(8, TILE, 8)) + square[:8]
                return carry

            lax.fori_loop(0, size // TILE, body, 0)
        out_ref[...] = jnp.sum(acc_ref[...], axis=0, keepdims=True)

    return pl.pallas_call(
        kernel,
        in_specs=[whole_vmem] * (n + 2),
        out_specs=[whole_vmem] * 2,
        out_shape=[
            jax.ShapeDtypeStruct((1, 2 * size), jnp.float32),
            jax.ShapeDtypeStruct((1, columns), jnp.float32),
        ],
        scratch_shapes=[pltpu.VMEM((1, 2 * size), jnp.float32), pltpu.VMEM((8, columns), jnp.float32)],
        compiler_params=params_of(4 * MIB),
        cost_estimate=cost(8 * size * columns, 4 * size * columns),
        name="early",
    )(gradient, row_moment, *messages)


def power_of(params):
    rows, columns = params.shape
    steps = rows // TILE
    shares = min(SHARES, steps)
    each = steps // shares

    def kernel(p_ref, *refs):
        *kept, o_ref, sems = refs
        copies = []
        for t in range(steps):
            here, there = pl.ds(t * TILE, TILE), pl.ds(t % each * TILE, TILE)
            copies.append(pltpu.make_async_copy(p_ref.at[here], kept[t // each].at[there], sems.at[t]))
            copies[-1].start()
        total = jnp.zeros((8, LANES), jnp.float32)
        for t in range(steps):
            copies[t].wait()

            def body(r, total):
                here = pl.ds(pl.multiple_of(t % each * TILE + r * 8, 8), 8)
                for k in range(columns // LANES):
                    p = kept[t // each][here, k * LANES : (k + 1) * LANES]
                    total = total + p * p
                return total

            total = lax.fori_loop(0, TILE // 8, body, total)
        o_ref[...] = total

    *kept, power = pl.pallas_call(
        kernel,
        in_specs=[anywhere],
        out_specs=[whole_vmem] * (shares + 1),
        out_shape=[pltpu.VMEM((rows // shares, columns), jnp.float32)] * shares
        + [jax.ShapeDtypeStruct((8, LANES), jnp.float32)],
        scratch_shapes=[pltpu.SemaphoreType.DMA((steps,))],
        compiler_params=params_of(MIB),
        cost_estimate=cost(2 * rows * columns, 4 * rows * columns),
        name="param_power",
    )(in_hbm(params))
    return kept, power


def tree(values):
    while len(values) > 1:
        values = [a + b for a, b in zip(values[::2], values[1::2])]
    return values[0]


def weigh(gradient, col_sums, col_moment, row_sums, early_sums, power, late):
    rows, columns = gradient.shape
    half = rows // 2
    chunks = columns // LANES
    n = len(col_sums)
    group = 4 * GROUP

    def kernel(g_ref, *refs):
        sums, refs = refs[:n], refs[n:]
        row_refs, refs = refs[:2], refs[2:]
        moment_ref, early_ref, power_ref, new_ref, root_ref, out_ref, wide_ref, acc_ref = refs
        total = tree([s[...] for s in sums]) + D * EPSILON
        new = DECAY * moment_ref[...] + (1.0 - DECAY) * total / D
        new_ref[...] = new
        root = lax.rsqrt(new)
        root_ref[...] = root
        wide_ref[...] = jnp.broadcast_to(root, wide_ref.shape)
        for h, row_ref in enumerate(row_refs):
            out_ref[:, h * late : (h + 1) * late] = row_ref[...]
        out_ref[:, 4 * late : 4 * late + LANES] = tree_lanes(early_ref[...] * (root * root), columns)
        out_ref[:, 4 * late + LANES :] = jnp.sum(power_ref[...], axis=0, keepdims=True)
        for h in range(2):

            def body(r, carry):
                here = pl.ds(pl.multiple_of(h * half + r * group, group), group)
                total = jnp.zeros((group, LANES), jnp.float32)
                for k in range(chunks):
                    lanes = slice(k * LANES, (k + 1) * LANES)
                    g = g_ref[here, lanes].astype(jnp.float32)
                    w = wide_ref[:, lanes]
                    g = jnp.concatenate([g[i : i + 8] * w for i in range(0, group, 8)], axis=0)
                    total = total + g * g
                acc_ref[pl.ds(pl.multiple_of(h * late + r * group, group), group), :] = total
                return carry

            lax.fori_loop(0, late // group, body, 0)
        for q in range(2 * late // LANES):
            lanes = slice(2 * late + q * LANES, 2 * late + (q + 1) * LANES)
            out_ref[:, lanes] = lane_sums(acc_ref[q * LANES : (q + 1) * LANES, :])

    return pl.pallas_call(
        kernel,
        in_specs=[whole_vmem] * (n + 6),
        out_specs=[whole_vmem] * 3,
        out_shape=[
            pltpu.VMEM((1, columns), jnp.float32),
            pltpu.VMEM((1, columns), jnp.float32),
            pltpu.VMEM((1, 4 * late + 2 * LANES), jnp.float32),
        ],
        scratch_shapes=[pltpu.VMEM((8, columns), jnp.float32), pltpu.VMEM((2 * late, LANES), jnp.float32)],
        compiler_params=params_of(4 * MIB),
        cost_estimate=cost(8 * late * columns, 4 * late * columns),
        name="weigh",
    )(gradient, *col_sums, *row_sums, col_moment, early_sums, power)


def balance(messages, row_moment, new_early, late):
    rows = row_moment.shape[1]
    half = rows // 2
    first = half - late
    n = len(messages)

    def kernel(*refs):
        got, (moment_ref, early_ref, new_ref, root_ref, out_ref) = refs[:n], refs[n:]
        total = tree([m[...] for m in got])
        ratio = jnp.zeros((1, LANES), jnp.float32)
        for h in range(2):
            here = slice(h * half, h * half + late)
            there = slice(h * late, (h + 1) * late)
            new = DECAY * moment_ref[:, here] + (1.0 - DECAY) * (total[:, there] + FF * EPSILON) / FF
            new_ref[:, here] = new
            new_ref[:, h * half + late : (h + 1) * half] = early_ref[:, h * first : (h + 1) * first]
            ratio = ratio + tree_lanes(total[:, (2 + h) * late : (3 + h) * late] / new, late)
        root_ref[...] = lax.rsqrt(new_ref[...])
        out_ref[...] = jnp.zeros_like(out_ref)
        out_ref[0:1, :] = ratio + total[:, 4 * late : 4 * late + LANES]
        out_ref[1:2, :] = tree_lanes(new_ref[...], rows)
        out_ref[2:3, :] = total[:, 4 * late + LANES :]

    return pl.pallas_call(
        kernel,
        in_specs=[whole_vmem] * (n + 2),
        out_specs=[whole_vmem] * 3,
        out_shape=[
            pltpu.VMEM((1, rows), jnp.float32),
            pltpu.VMEM((1, rows), jnp.float32),
            pltpu.VMEM((8, LANES), jnp.float32),
        ],
        compiler_params=params_of(4 * MIB),
        name="balance",
    )(*messages, row_moment, new_early)


def tree_lanes(x, rows):
    total = x[:, :LANES]
    for q in range(1, rows // LANES):
        total = total + x[:, q * LANES : (q + 1) * LANES]
    return total


def finish(gradient, params, row_root, col_root, stats):
    rows, columns = gradient.shape
    n = len(stats)
    shares = len(params)
    each = rows // shares // TILE
    group = 2 * GROUP

    def kernel(_, row_ref, col_ref, *refs):
        got, refs = refs[shares : shares + n], refs[shares + n :]
        g_ref, held, (new_ref, update_ref, scale_ref, sems, first_sems) = refs[0], refs[1 : 1 + shares], refs[1 + shares :]
        total = jnp.sum(tree([s[...] for s in got]), axis=1, keepdims=True)
        mean = total[1:2] / D
        rms = jnp.sqrt(mean * total[0:1] / (D * FF))
        scale = jnp.sqrt(total[2:3] / (D * FF))
        factor = scale * jnp.sqrt(mean) / jnp.maximum(1.0, rms)
        scale_ref[...] = jnp.broadcast_to(col_ref[...] * factor, scale_ref.shape)

        def copies(q, t):
            here = pl.ds(pl.multiple_of((q * each + t) * TILE, TILE), TILE)
            there = pl.ds(pl.multiple_of(t * TILE, TILE), TILE)
            return (
                pltpu.make_async_copy(held[q].at[there], new_ref.at[here], sems.at[0, q * each + t]),
                pltpu.make_async_copy(g_ref.at[here], update_ref.at[here], sems.at[1, q * each + t]),
            )

        def opening(r):
            here = pl.ds(r * group, group)
            return (
                pltpu.make_async_copy(held[0].at[here], new_ref.at[here], first_sems.at[0, r]),
                pltpu.make_async_copy(g_ref.at[here], update_ref.at[here], first_sems.at[1, r]),
            )

        def rows_of(q, t, wide, r):
            here = pl.ds(pl.multiple_of((q * each + t) * TILE + r * group, group), group)
            there = pl.ds(pl.multiple_of(t * TILE + r * group, group), group)
            root = wide[r * group : (r + 1) * group, :]
            for k in range(columns // LANES):
                at = slice(k * LANES, (k + 1) * LANES)
                g = g_ref[here, at].astype(jnp.float32)
                s = scale_ref[:, at]
                full = jnp.concatenate([g[i : i + 8] * s for i in range(0, group, 8)], axis=0) * root
                g_ref[here, at] = full.astype(g_ref.dtype)
                held[q][there, at] = held[q][there, at] - LEARN_RATE * full

        def widen(q, t):
            lanes = row_ref[:, pl.ds(pl.multiple_of((q * each + t) * TILE, TILE), TILE)]
            return jnp.broadcast_to(lanes, (LANES, TILE)).T

        wide = widen(0, 0)
        for r in range(TILE // group):
            rows_of(0, 0, wide, r)
            for copy in opening(r):
                copy.start()

        for q in range(shares):

            def block(t, carry):
                wide = widen(q, t)
                for r in range(TILE // group):
                    rows_of(q, t, wide, r)
                for copy in copies(q, t):
                    copy.start()
                return carry

            lax.fori_loop(0 if q else 1, each, block, 0)

        for r in range(TILE // group):
            for copy in opening(r):
                copy.wait()
        for q in range(shares):

            def drain(t, carry):
                for copy in copies(q, t):
                    copy.wait()
                return carry

            lax.fori_loop(0 if q else 1, each, drain, 0)

    out = pl.pallas_call(
        kernel,
        in_specs=[anywhere, whole_vmem, whole_vmem] + [anywhere] * shares + [whole_vmem] * n,
        out_specs=[whole_vmem] * (1 + shares) + [anywhere] * 2,
        out_shape=[pltpu.VMEM(x.shape, x.dtype) for x in (gradient, *params)]
        + [pltpu.HBM((rows, columns), jnp.float32), pltpu.HBM((rows, columns), jnp.bfloat16)],
        input_output_aliases={0: 0, **{3 + q: 1 + q for q in range(shares)}},
        scratch_shapes=[
            pltpu.VMEM((8, columns), jnp.float32),
            pltpu.SemaphoreType.DMA((2, rows // TILE)),
            pltpu.SemaphoreType.DMA((2, TILE // group)),
        ],
        compiler_params=params_of(4 * MIB),
        cost_estimate=cost(6 * rows * columns, 12 * rows * columns),
        name="finish",
    )(gradient, row_root, col_root, *params, *stats)
    return out[-2:]


def all_parts(value, axis, size):
    return [value] + [lax.ppermute(value, axis, pairs(size, k)) for k in range(1, size)]


def cut(half):
    units = half // TILE
    late = 2 if units > 3 else 1
    first = (units - late + 1) // 2 if units > 3 else units - late
    edges = [((units - first) * TILE, first * TILE)]
    if units - first > late:
        edges.append((late * TILE, (units - first - late) * TILE))
    return edges + [(0, late * TILE)]


def after(values, others):
    return lax.optimization_barrier((tuple(values), tuple(others)))[0]


def solution(mesh):
    across = mesh.shape["row"]
    along = mesh.shape["col"]

    def hop(values, lines):
        return [lax.ppermute(v, "dp", pairs(mesh.shape["dp"], n)) for v, n in zip(values, lines)]

    def on_device(grad_parts, params, row_moment, col_moment):
        parts = grad_parts[0]
        rows, columns = parts.shape[1:]
        half = rows // 2
        me = lax.axis_index("dp").astype(jnp.int32)[None]

        held = in_hbm(parts)
        pieces = cut(half)
        late = pieces[-1][1]
        rounds = []

        def send(values, lines):
            if len(rounds) > 1:
                values = after(values, rounds[-2])
            rounds.append(hop(values, lines))
            return rounds[-1]

        picked = grab(held, [(3, 0), (3, half)], TILE)
        (turn,) = after([me], picked)
        head = send(picked, NEAR)
        picked = pick(held, turn, [(3, TILE), (3, half + TILE)], half - TILE)
        (turn,) = after([me], picked)
        rest = send(picked, NEAR)
        second = send(pick(held, turn, [(NEAR[0], 0), (NEAR[1], half)], half), NEAR)

        third, done = [], []
        for at, size in pieces:
            if at:
                done = merge(held, me, after(rest, done), at, TILE, size)
            elif size == TILE:
                done = merge(held, me, after(head, done), 0, 0, size)
            else:
                done = merge(held, me, after(rest, done), 0, TILE, size, after(head, done))
            third.append(send(done, FAR))

        state, row_pieces = None, {}
        for i, ((at, size), came) in enumerate(zip(pieces[:-1], third)):
            if i + 2 == len(pieces):
                kept, power = power_of(after([params[0]], state[1:] if state else second)[0])
                base = presum(held, me, second, 0, late)
                came = after(came, [*kept, base])
            *state, row_pieces[at] = settle(held, me, second, came, at, size, state, 64)
        message = jnp.concatenate(
            [row_pieces[at][:, h * size : (h + 1) * size] for h in range(2) for at, size in sorted(pieces[:-1])], axis=1
        )
        new_early, early_sums = early(state[0], all_parts(message, "col", along), row_moment, late, half - late)
        gradient, col_sums, last_rows = close(base, third[-1][1], 1, *state)
        gradient, col_sums, first_rows = close(base, third[-1][0], 0, gradient, col_sums)

        col_parts = all_parts(col_sums, "row", across)
        new_col, col_root, message = weigh(gradient, col_parts, col_moment, [first_rows, last_rows], early_sums, power, late)
        new_row, row_root, stats = balance(all_parts(message, "col", along), row_moment, new_early, late)
        new_params, update = finish(gradient, kept, row_root, col_root, all_parts(stats, "row", across))
        return new_params[None], update[None], new_row, new_col

    placed = (P("dp", None, "row", "col"), P("dp", "row", "col"), P("dp", "row"), P("dp", "col"))
    return jax.shard_map(
        on_device,
        mesh=mesh,
        in_specs=placed,
        out_specs=(P("dp", "row", "col"), P("dp", "row", "col"), P("dp", "row"), P("dp", "col")),
        check_vma=False,
    )
```
